256 devices in a mesh: gx: 8 (over y, core), gy: 32 (over x, z).
Axes of the slice: x: 4, y: 4, z: 8, core: 2. Of those that a mesh axis runs over, the one named last changes fastest.
Arguments:
- right_side: float32 [2048, 8, 64], P(('gx', 'gy')), may hold values from -6 to 6
- operator_top: float32 [2048, 27, 64, 64], P(('gx', 'gy')), may hold values from -0.078125 to 0.078125
- columns_top: int32 [2048, 27], P(('gx', 'gy')), may hold values from 0 to 2047, as said below
- aggregate_top: int32 [2048], P(('gx', 'gy')), may hold values from 0 to 1023, as said below
- prolong_top: float32 [2048, 64, 64], P(('gx', 'gy')), may hold values from -0.75 to 0.75
- operator_mid: float32 [1024, 27, 64, 64], P(('gx', 'gy')), may hold values from -0.078125 to 0.078125
- columns_mid: int32 [1024, 27], P(('gx', 'gy')), may hold values from 0 to 1023, as said below
- aggregate_mid: int32 [1024], P(('gx', 'gy')), may hold values from 0 to 511, as said below
- prolong_mid: float32 [1024, 64, 64], P(('gx', 'gy')), may hold values from -0.75 to 0.75
- operator_low: float32 [512, 27, 64, 64], P(('gx', 'gy')), may hold values from -0.078125 to 0.078125
- columns_low: int32 [512, 27], P(('gx', 'gy')), may hold values from 0 to 511, as said below
Outputs:
- correction: float32 [2048, 8, 64], P(('gx', 'gy'))
- smoothed_residual: float32 [2048, 8, 64], P(('gx', 'gy'))
The draws below stay inside these ranges and needn't reach their ends.
Inputs may be any that keep to these rules, and one draw needn't show every extreme that they name: `columns_top`: slot 0 of block row b names b itself; every column of block row b lies on the device of b or on its first level partner. `columns_mid`: slot 0 of block row b names b itself; every column of block row b lies on the device of b or on its second level partner. `columns_low`: slot 0 of block row b names b itself; every column of block row b lies on the device of b or on its third level partner. `aggregate_top`: block row b joins a second level block of the device of b or of its first level partner; counts per block are uneven. `aggregate_mid`: block row b joins a third level block of the device of b or of its second level partner; counts per block are uneven.
All inputs are finite; a program needn't handle non-finite values.
Results may differ from the reference program's by a relative error of at most 0.0001.
Values sent between devices are 32-bit elements; how exact they have to be, the bound alone decides.
No kernel may reach another device: no remote copies, remote signals or barrier semaphores. Data moves between devices by JAX's collectives and lax.ppermute only.
A program may use at most 64 MiB of HBM per device.

```python
import jax
import jax.numpy as jnp
from jax import lax

DOFS = 64
NEIGHBORS = 27
SOURCES = 8
ROWS_TOP = 8
ROWS_MID = 4
ROWS_LOW = 2
BLOCKS_TOP = 2048
BLOCKS_MID = 1024
BLOCKS_LOW = 512
N_GX = 8
N_GY = 32


def column_draw(key, rows, mask):
    total = rows * N_GX * N_GY
    block = jnp.arange(total, dtype=jnp.int32)
    device = block // rows
    partner = jnp.bitwise_xor(device, mask)
    pick = jax.random.randint(key, (total, NEIGHBORS - 1), 0, 2 * rows, dtype=jnp.int32)
    others = jnp.where(pick < rows, device[:, None] * rows + pick, partner[:, None] * rows + pick - rows)
    return jnp.concatenate([block[:, None], others], axis=1).astype(jnp.int32)


def aggregate_draw(key, rows, mask):
    total = rows * N_GX * N_GY
    half_rows = rows // 2
    block = jnp.arange(total, dtype=jnp.int32)
    device = block // rows
    partner = jnp.bitwise_xor(device, mask)
    pick = jax.random.randint(key, (total,), 0, rows, dtype=jnp.int32)
    return jnp.where(pick < half_rows, device * half_rows + pick, partner * half_rows + pick - half_rows).astype(jnp.int32)


def draw_columns_top(key, part):
    key = jax.random.fold_in(key, 11)
    return column_draw(key, ROWS_TOP, N_GY // 2)


def draw_columns_mid(key, part):
    key = jax.random.fold_in(key, 12)
    return column_draw(key, ROWS_MID, N_GX // 2 * N_GY)


def draw_columns_low(key, part):
    key = jax.random.fold_in(key, 13)
    return column_draw(key, ROWS_LOW, N_GY // 4)


def draw_aggregate_top(key, part):
    key = jax.random.fold_in(key, 14)
    return aggregate_draw(key, ROWS_TOP, N_GY // 2)


def draw_aggregate_mid(key, part):
    key = jax.random.fold_in(key, 15)
    return aggregate_draw(key, ROWS_MID, N_GX // 2 * N_GY)


def shard_levels(key, shape, cuts, least, top_value):
    loudness, own = 1.0, jax.random.fold_in(key, 6)
    for axis_at, parts in cuts:
        draws = jnp.exp(jax.random.uniform(jax.random.fold_in(own, axis_at), (parts,), jnp.float32, least / len(cuts), top_value / len(cuts)))
        loudness = loudness * jnp.repeat(draws, shape[axis_at] // parts).reshape([-1 if axis == axis_at else 1 for axis in range(len(shape))])
    return loudness


def noise(stream_key, dims, deviation, reach, cuts=(), kind=jnp.bfloat16):
    values = jax.random.normal(stream_key, dims, jnp.float32) * deviation
    if len(cuts) > 0:
        values = shard_levels(stream_key, dims, cuts, -0.22, 0.18) * values
    return jnp.clip(values, min=-reach, max=reach).astype(kind)


def setup_inputs(seed: int = 0) -> dict:
    key_list = jax.random.split(jax.random.key(seed), 12)
    right_side = noise(key_list[0], (BLOCKS_TOP, SOURCES, DOFS), 1.0, 6.0, ((0, 256),), jnp.float32)
    operator_top = noise(key_list[1], (BLOCKS_TOP, NEIGHBORS, DOFS, DOFS), (4 * NEIGHBORS * DOFS) ** -0.5, 0.078125, ((0, 256),), jnp.float32)
    columns_top = draw_columns_top(jax.random.fold_in(key_list[11], 71), 0)
    aggregate_top = draw_aggregate_top(jax.random.fold_in(key_list[11], 71), 0)
    prolong_top = noise(key_list[4], (BLOCKS_TOP, DOFS, DOFS), DOFS ** -0.5, 0.75, ((0, 256),), jnp.float32)
    operator_mid = noise(key_list[5], (BLOCKS_MID, NEIGHBORS, DOFS, DOFS), (4 * NEIGHBORS * DOFS) ** -0.5, 0.078125, ((0, 256),), jnp.float32)
    columns_mid = draw_columns_mid(jax.random.fold_in(key_list[11], 71), 0)
    aggregate_mid = draw_aggregate_mid(jax.random.fold_in(key_list[11], 71), 0)
    prolong_mid = noise(key_list[8], (BLOCKS_MID, DOFS, DOFS), DOFS ** -0.5, 0.75, ((0, 256),), jnp.float32)
    operator_low = noise(key_list[9], (BLOCKS_LOW, NEIGHBORS, DOFS, DOFS), (4 * NEIGHBORS * DOFS) ** -0.5, 0.078125, ((0, 256),), jnp.float32)
    columns_low = draw_columns_low(jax.random.fold_in(key_list[11], 71), 0)
    return {"right_side": right_side, "operator_top": operator_top, "columns_top": columns_top, "aggregate_top": aggregate_top, "prolong_top": prolong_top, "operator_mid": operator_mid, "columns_mid": columns_mid, "aggregate_mid": aggregate_mid, "prolong_mid": prolong_mid, "operator_low": operator_low, "columns_low": columns_low}


center = 1.0
half_width = 0.6


def apply_operator(operator, columns, vector):
    blocks = vector.shape[0]
    group = min(blocks, 256)
    count = blocks // group
    ops = operator.reshape((count, group, operator.shape[1], operator.shape[2], operator.shape[3]))
    cols = columns.reshape((count, group, columns.shape[1]))
    owns = vector.reshape((count, group, vector.shape[1], vector.shape[2]))

    def one_group(pieces):
        block_ops, block_cols, block_own = pieces
        gathered = vector[block_cols]
        return block_own + jnp.einsum("bjik,bjsk->bsi", block_ops, gathered, precision=lax.Precision.HIGHEST)

    result = lax.map(one_group, (ops, cols, owns))
    return result.reshape(vector.shape)


def chebyshev(operator, columns, residual):
    sigma = center / half_width
    rho = half_width / center
    solution = jnp.zeros_like(residual)
    direction = residual / center
    for step in range(3):
        solution = solution + direction
        residual = residual - apply_operator(operator, columns, direction)
        rho_next = 1.0 / (2.0 * sigma - rho)
        direction = rho_next * rho * direction + (2.0 * rho_next / half_width) * residual
        rho = rho_next
    return solution, residual


def restrict(prolong, aggregate, residual, coarse):
    terms = jnp.einsum("bki,bsk->bsi", prolong, residual, precision=lax.Precision.HIGHEST)
    return jax.ops.segment_sum(terms, aggregate, num_segments=coarse)


def prolongate(prolong, aggregate, fine, coarse_values):
    picked = coarse_values[aggregate]
    return fine + jnp.einsum("bik,bsk->bsi", prolong, picked, precision=lax.Precision.HIGHEST)


def reference(right_side, operator_top, columns_top, aggregate_top, prolong_top, operator_mid, columns_mid, aggregate_mid, prolong_mid, operator_low, columns_low):
    x_top, smoothed = chebyshev(operator_top, columns_top, right_side)
    mid_side = restrict(prolong_top, aggregate_top, smoothed, BLOCKS_MID)
    x_mid, r_mid = chebyshev(operator_mid, columns_mid, mid_side)
    low_side = restrict(prolong_mid, aggregate_mid, r_mid, BLOCKS_LOW)
    x_low, r_low = chebyshev(operator_low, columns_low, low_side)
    mid_fixed = prolongate(prolong_mid, aggregate_mid, x_mid, x_low)
    correction = prolongate(prolong_top, aggregate_top, x_top, mid_fixed)
    return correction, smoothed
```

```python
import functools

import jax
import jax.numpy as jnp
from jax import lax
from jax.experimental import pallas as pl
from jax.experimental.pallas import tpu as pltpu
from jax.sharding import PartitionSpec as P

center = 1.0
half_width = 0.6
F32 = jnp.float32
BF16 = jnp.bfloat16
N = 64
S = 8
J = 27


def chebyshev_weights():
    sigma = center / half_width
    rho = half_width / center
    weights = []
    for step in range(3):
        rho_next = 1.0 / (2.0 * sigma - rho)
        weights.append((rho_next * rho, 2.0 * rho_next / half_width))
        rho = rho_next
    return weights


W = chebyshev_weights()
COST = {"pack_side": 20000, "prepare_top": 4000, "step_second": 100000, "step_third": 6000, "add_mid": 6000}


def call(name, body, outs, *args, scalars=0):
    spaces = [pltpu.SMEM] * scalars + [pltpu.VMEM] * (len(args) - scalars)
    args = [pltpu.with_memory_space_constraint(a, m) for a, m in zip(args, spaces)]
    return pl.pallas_call(
        body,
        name=name,
        out_shape=[pltpu.VMEM(shape, dtype) for shape, dtype in outs],
        in_specs=[pl.BlockSpec(memory_space=m) for m in spaces],
        out_specs=[pl.BlockSpec(memory_space=pltpu.VMEM)] * len(outs),
        cost_estimate=pl.CostEstimate(flops=COST.get(name, 200) * 1000000, bytes_accessed=0, transcendentals=0),
        compiler_params=pltpu.CompilerParams(vmem_limit_bytes=8 * 1024 * 1024),
    )(*args)


def split(value):
    high = value.astype(BF16)
    return high, (value - high.astype(F32)).astype(BF16)


def stack(value):
    return jnp.concatenate(split(value), axis=0)


def fold(value):
    return value[:S] + value[S:]


def apply_t(vector, matrix):
    both = stack(vector)
    both = jnp.concatenate([both, both], axis=1)
    out = lax.dot_general(both, matrix, (((1,), (1,)), ((), ())), preferred_element_type=F32)
    return fold(out)


def apply_n(vector, matrix):
    out = fold(lax.dot_general(stack(vector), matrix, (((1,), (0,)), ((), ())), preferred_element_type=F32))
    half = out.shape[1] // 2
    return out[:, :half] + out[:, half:]


def pack(ref):
    return jnp.concatenate([ref[b] for b in range(ref.shape[0])], axis=1)


def unpack(value, ref):
    for b in range(ref.shape[0]):
        ref[b] = value[:, b * N : (b + 1) * N]


def local(index, rows, device):
    return (index % rows) + jnp.where(index // rows == device, 0, rows)


def collapse_rows(cols, b, rows, device, blocks, sums):
    for part in sums:
        part[...] = jnp.zeros(part.shape, F32)
    for j in range(J):
        for n, part in enumerate(sums):
            at = local(cols[b + n, j], rows, device)
            part[at] = part[at] + blocks[b + n, j]


def pair_of(sums, at):
    return jnp.concatenate([sums[at], sums[at + 1]], axis=1)


def spread_row(agg, b, rows, device, prolong):
    at = local(agg[b], rows, device)
    block = prolong[b]
    twice = jnp.concatenate([block, block], axis=1)
    lane = lax.broadcasted_iota(jnp.int32, (N, 2 * N), 1) // N
    return [jnp.where(lane + 2 * piece == at, twice, 0.0) for piece in range(rows)]


def put_halves(ref, rows_at, pieces):
    half = len(pieces) // 2
    width = half * 2 * N
    for p, piece in enumerate(pieces):
        high, low = split(piece)
        base = (p // half) * 2 * width + (p % half) * 2 * N
        ref[rows_at, pl.ds(base, 2 * N)] = high
        ref[rows_at, pl.ds(base + width, 2 * N)] = low


def pack_side(side, out):
    out[...] = pack(side)


def lanes_of(b):
    return pl.ds(pl.multiple_of(b * N, N), N)


def prepare_top(cols, blocks, first, matrix, product, *sums):
    rows = blocks.shape[0]
    device = cols[0, 0] // rows

    def some(step, carry):
        b = step * len(sums)
        collapse_rows(cols, b, rows, device, blocks, sums)
        for n, part in enumerate(sums):
            put_halves(matrix, lanes_of(b + n), [pair_of(part, 2 * c) for c in range(rows)])
        return carry

    lax.fori_loop(0, rows // len(sums), some, 0)
    product[...] = apply_t(first[...], matrix[:, : 2 * rows * N])


def collapse_out(cols, blocks, out, sums):
    rows = blocks.shape[0]
    device = cols[0, 0] // rows
    sums = [part.at[: 2 * rows] for part in sums]

    def some(step, carry):
        b = step * len(sums)
        collapse_rows(cols, b, rows, device, blocks, sums)
        for n, part in enumerate(sums):
            for c in range(rows):
                out[lanes_of(b + n), pl.ds(c * 2 * N, 2 * N)] = pair_of(part, 2 * c)
        return carry

    lax.fori_loop(0, rows // len(sums), some, 0)
    return device


def shadow_second(cols, agg, blocks, prolong, direction, matrix, product, send, *sums):
    own_product(direction, matrix, product)
    rows = blocks.shape[0]
    device = collapse_out(cols, blocks, send, sums)
    for b in range(rows):
        for p, piece in enumerate(spread_row(agg, b, rows // 2, device, prolong)):
            send[b * N : (b + 1) * N, (rows + p) * 2 * N : (rows + p + 1) * 2 * N] = piece


def shadow_third(cols, cols_top, agg_top, blocks, prolong_top, direction, matrix, product, send, transfer, *sums):
    own_product(direction, matrix, product)
    collapse_out(cols, blocks, send, sums)
    rows = prolong_top.shape[0]
    device = cols_top[0, 0] // rows
    for b in range(rows):
        put_halves(transfer, slice(b * N, (b + 1) * N), spread_row(agg_top, b, rows // 2, device, prolong_top))


def own_product(vector, matrix, product):
    product[...] = apply_t(vector[...], matrix[:, : matrix.shape[1] // 2])


def other_product(product, other, matrix):
    return product[...] + apply_t(other, matrix[:, matrix.shape[1] // 2 :])


def step_first(first, product, other, matrix, direction, residual):
    d = first[...]
    r = d - (d + other_product(product, other[...], matrix))
    residual[...] = r
    direction[...] = W[0][0] * d + W[0][1] * r


def step_second(first, old, residual, product, other, matrix, direction, new_residual, total):
    d = old[...]
    r = residual[...] - (d + other_product(product, other[...], matrix))
    new_residual[...] = r
    new = W[1][0] * d + W[1][1] * r
    direction[...] = new
    total[...] = first[...] + d + new


def step_third(old, residual, product, other, matrix, transfer, new_residual, own_part, other_part):
    r = residual[...] - (old[...] + other_product(product, other[...], matrix))
    new_residual[...] = r
    half = transfer.shape[1] // 2
    other_part[...] = apply_n(r, transfer[:, half:])
    own_part[...] = apply_n(r, transfer[:, :half])


def add(a, b, out):
    out[...] = a[...] + b[...]


def write_blocks(value, out):
    unpack(value[...], out)


def swapped(value):
    half = value.shape[1] // 2
    return jnp.concatenate([value[:, half:], value[:, :half]], axis=1)


def join_mid(own, other, matrix, transfer):
    rows = own.shape[0]
    width = 2 * rows
    for at, source, turn in ((0, own, False), (1, other, True)):
        value = source[:, :width]
        shift = source[:, width:]
        if turn:
            value, shift = swapped(value), swapped(shift)
        here = pl.ds(at * rows, rows)
        for side in range(2):
            high, low = split(value[:, side * rows : (side + 1) * rows])
            matrix[here, pl.ds(2 * side * rows, rows)] = high
            matrix[here, pl.ds((2 * side + 1) * rows, rows)] = low
        high, low = split(shift)
        transfer[here, pl.ds(0, rows)] = high
        transfer[here, pl.ds(rows, rows)] = low


def join_low(own, other, out):
    rows = own.shape[0]
    out[:rows] = own[...]
    out[rows:] = swapped(other[...])


def split_low(own, other, out_own, out_other):
    width = own.shape[1]
    for source, out in ((own, out_own), (other, out_other)):
        high, low = split(source[...])
        out[:, :width] = high
        out[:, width:] = low


def solve_mid(product, own, other, matrix, transfer, low_pair, solution):
    half = own.shape[1]
    d = jnp.concatenate([own[...], other[...]], axis=1)
    r = d - (d + other_product(product, other[...], matrix))
    x = d[:, :half]
    for step in range(2):
        d = W[step][0] * d + W[step][1] * r
        x = x + d[:, :half]
        mid = matrix.shape[1] // 2
        r = r - (d + apply_t(d[:, :half], matrix[:, :mid]) + apply_t(d[:, half:], matrix[:, mid:]))
    solution[...] = x
    low_pair[...] = apply_n(r, transfer[...])


def solve_low(own, other, matrix_own, matrix_other, fine, transfer, fixed):
    half = own.shape[1] // 2
    found = []
    for at, matrix in ((0, matrix_own), (1, matrix_other)):
        here = slice(at * half, (at + 1) * half)
        d = jnp.concatenate([own[:, here], other[:, here]], axis=1)
        r = d
        x = d
        for step in range(2):
            r = r - (d + apply_t(d, matrix[...]))
            d = W[step][0] * d + W[step][1] * r
            x = x + d
        found.append(x[:, :half])
    fixed[...] = fine[...] + apply_t(jnp.concatenate(found, axis=1), transfer[: fixed.shape[1]])


def start_correction(total, fixed, transfer, out):
    out[...] = total[...] + apply_t(fixed[...], transfer[:, : transfer.shape[1] // 2])


def end_correction(partial, other, transfer, out):
    unpack(other_product(partial, other[...], transfer), out)


def per_device(
    flips,
    right_side,
    operator_top,
    columns_top,
    aggregate_top,
    prolong_top,
    operator_mid,
    columns_mid,
    aggregate_mid,
    prolong_mid,
    operator_low,
    columns_low,
):
    def flip(value, level):
        return lax.ppermute(value, ("gx", "gy"), flips[level])

    rows = operator_top.shape[0]
    n_top = rows * N
    n_mid = n_top // 2
    n_low = n_mid // 2
    vec_top = ((S, n_top), F32)
    vec_mid = ((S, n_mid), F32)
    sums = [pltpu.VMEM((2 * rows, N, N), F32)] * 2

    (first,) = call("pack_side", pack_side, [vec_top], right_side)
    other = flip(first, 0)
    matrix, product = prepare(
        "prepare_top",
        prepare_top,
        [((n_top, 4 * n_top), BF16), vec_top],
        sums,
        1,
        columns_top,
        operator_top,
        first,
    )
    d1, r1 = call("step_first", step_first, [vec_top, vec_top], first, product, other, matrix)
    other = flip(d1, 0)
    product, send_mid = prepare(
        "shadow_second",
        shadow_second,
        [vec_top, ((n_mid, 3 * n_mid), F32)],
        sums,
        2,
        columns_mid,
        aggregate_mid,
        operator_mid,
        prolong_mid,
        d1,
        matrix,
    )
    mid_other = flip(send_mid, 1)
    d2, r2, total = call("step_second", step_second, [vec_top] * 3, first, d1, r1, product, other, matrix)
    other = flip(d2, 0)
    product, send_low, transfer = prepare(
        "shadow_third",
        shadow_third,
        [vec_top, ((n_low, 2 * n_low), F32), ((n_top, 4 * n_mid), BF16)],
        sums,
        3,
        columns_low,
        columns_top,
        aggregate_top,
        operator_low,
        prolong_top,
        d2,
        matrix,
    )
    low_other = flip(send_low, 2)
    smoothed, own_part, other_part = call(
        "step_third", step_third, [vec_top, vec_mid, vec_mid], d2, r2, product, other, matrix, transfer
    )
    arrived = flip(other_part, 0)
    (low_matrix,) = call("join_low", join_low, [((2 * n_low, 2 * n_low), F32)], send_low, low_other)
    low_matrix_other = flip(low_matrix, 1)
    (smoothed_blocks,) = call("write_smoothed", write_blocks, [((rows, S, N), F32)], smoothed)
    (mid_side,) = call("add_mid", add, [vec_mid], own_part, arrived)
    other = flip(mid_side, 1)
    mid_matrix, mid_transfer = call(
        "join_mid", join_mid, [((2 * n_mid, 4 * n_mid), BF16), ((2 * n_mid, 4 * n_low), BF16)], send_mid, mid_other
    )
    (product,) = call("own_mid", own_product, [vec_top], mid_side, mid_matrix)
    low_pair, x_mid = call(
        "solve_mid", solve_mid, [((S, 2 * n_low), F32), vec_mid], product, mid_side, other, mid_matrix, mid_transfer
    )
    other = flip(low_pair, 2)
    low_own, low_far = call(
        "split_low", split_low, [((2 * n_low, 4 * n_low), BF16)] * 2, low_matrix, low_matrix_other
    )
    (mid_fixed,) = call("solve_low", solve_low, [vec_mid], low_pair, other, low_own, low_far, x_mid, mid_transfer)
    other = flip(mid_fixed, 0)
    (partial,) = call("start_correction", start_correction, [vec_top], total, mid_fixed, transfer)
    (correction,) = call("end_correction", end_correction, [((rows, S, N), F32)], partial, other, transfer)
    return correction, smoothed_blocks


def prepare(name, body, outs, scratch, scalars, *args):
    spaces = [pltpu.SMEM] * scalars + [pltpu.VMEM] * (len(args) - scalars)
    args = [pltpu.with_memory_space_constraint(a, m) for a, m in zip(args, spaces)]
    return pl.pallas_call(
        body,
        name=name,
        out_shape=[pltpu.VMEM(shape, dtype) for shape, dtype in outs],
        in_specs=[pl.BlockSpec(memory_space=m) for m in spaces],
        out_specs=[pl.BlockSpec(memory_space=pltpu.VMEM)] * len(outs),
        scratch_shapes=scratch,
        cost_estimate=pl.CostEstimate(flops=COST.get(name, 200) * 1000000, bytes_accessed=0, transcendentals=0),
        compiler_params=pltpu.CompilerParams(vmem_limit_bytes=8 * 1024 * 1024),
    )(*args)


def solution(mesh):
    n_gx, n_gy = mesh.shape["gx"], mesh.shape["gy"]
    masks = (n_gy // 2, n_gx // 2 * n_gy, n_gy // 4)
    flips = [[(source, source ^ mask) for source in range(n_gx * n_gy)] for mask in masks]
    lead = ("gx", "gy")
    in_specs = (
        P(lead, None, None),
        P(lead, None, None, None),
        P(lead, None),
        P(lead),
        P(lead, None, None),
        P(lead, None, None, None),
        P(lead, None),
        P(lead),
        P(lead, None, None),
        P(lead, None, None, None),
        P(lead, None),
    )
    out_specs = (P(lead, None, None), P(lead, None, None))
    return jax.shard_map(
        functools.partial(per_device, flips), mesh=mesh, in_specs=in_specs, out_specs=out_specs, check_vma=False
    )
```

```python
import functools

import jax
import jax.numpy as jnp
from jax import lax
from jax.experimental import pallas as pl
from jax.experimental.pallas import tpu as pltpu
from jax.sharding import PartitionSpec as P

center = 1.0
half_width = 0.6
F32 = jnp.float32
BF16 = jnp.bfloat16
N = 64
S = 8
J = 27


def chebyshev_weights():
    sigma = center / half_width
    rho = half_width / center
    weights = []
    for step in range(3):
        rho_next = 1.0 / (2.0 * sigma - rho)
        weights.append((rho_next * rho, 2.0 * rho_next / half_width))
        rho = rho_next
    return weights


W = chebyshev_weights()
COST = {"prepare_top": 4000, "step_first": 4000, "step_second": 100000, "step_third": 6000, "solve_mid": 20000}


def call(name, body, outs, *args, remote=(), scratch=(), aliases=None, limit=8):
    spaces = [pltpu.HBM if at in remote else pltpu.VMEM for at in range(len(args))]
    args = [pltpu.with_memory_space_constraint(a, m) for a, m in zip(args, spaces)]
    return pl.pallas_call(
        body,
        name=name,
        out_shape=[pltpu.VMEM(shape, dtype) for shape, dtype in outs],
        in_specs=[pl.BlockSpec(memory_space=m) for m in spaces],
        out_specs=[pl.BlockSpec(memory_space=pltpu.VMEM)] * len(outs),
        scratch_shapes=scratch,
        input_output_aliases=aliases or {},
        cost_estimate=pl.CostEstimate(flops=COST.get(name, 200) * 1000000, bytes_accessed=0, transcendentals=0),
        compiler_params=pltpu.CompilerParams(vmem_limit_bytes=limit * 1024 * 1024),
    )(*args)


def copies(sources, targets, sems):
    moves = [pltpu.make_async_copy(s, t, sems.at[n]) for n, (s, t) in enumerate(zip(sources, targets))]
    for move in moves:
        move.start()

    def wait():
        for move in moves:
            move.wait()

    return wait


def index_scratch(*arrays):
    return [pltpu.SemaphoreType.DMA((len(arrays),))] + [pltpu.SMEM(a.shape, jnp.int32) for a in arrays]


def split(value):
    high = value.astype(BF16)
    return high, (value - high.astype(F32)).astype(BF16)


def stack(value):
    return jnp.concatenate(split(value), axis=0)


def fold(value):
    return value[:S] + value[S:]


def apply_t(vector, matrix):
    both = stack(vector)
    both = jnp.concatenate([both, both], axis=1)
    out = lax.dot_general(both, matrix, (((1,), (1,)), ((), ())), preferred_element_type=F32)
    return fold(out)


def apply_n(vector, matrix):
    out = fold(lax.dot_general(stack(vector), matrix, (((1,), (0,)), ((), ())), preferred_element_type=F32))
    half = out.shape[1] // 2
    return out[:, :half] + out[:, half:]


def pack(ref):
    return jnp.concatenate([ref[b] for b in range(ref.shape[0])], axis=1)


def unpack(value, ref):
    for b in range(ref.shape[0]):
        ref[b] = value[:, b * N : (b + 1) * N]


def local(index, rows, device):
    offset = index ^ (device * rows)
    return jnp.minimum(offset, rows + (offset & (rows - 1)))


def collapse_rows(cols, b, rows, device, blocks, sums):
    for part in sums:
        part[...] = jnp.zeros(part.shape, F32)
    for j in range(J):
        for n, part in enumerate(sums):
            at = local(cols[b + n, j], rows, device)
            part[at] = part[at] + blocks[b + n, j]


def pair_of(sums, at):
    return jnp.concatenate([sums[at], sums[at + 1]], axis=1)


def spread(at, rows, block):
    twice = jnp.concatenate([block, block], axis=1)
    lane = lax.broadcasted_iota(jnp.int32, (N, 2 * N), 1) // N
    return [jnp.where(lane + 2 * piece == at, twice, 0.0) for piece in range(rows)]


def put_halves(ref, rows_at, pieces):
    half = len(pieces) // 2
    width = half * 2 * N
    for p, piece in enumerate(pieces):
        high, low = split(piece)
        base = (p // half) * 2 * width + (p % half) * 2 * N
        ref[rows_at, pl.ds(base, 2 * N)] = high
        ref[rows_at, pl.ds(base + width, 2 * N)] = low


def lanes_of(b):
    return pl.ds(pl.multiple_of(b * N, N), N)


def prepare_top(cols_in, side_in, remote, matrix, first, product, small, cols, side, held, sems, *sums):
    rows = remote.shape[0]
    wait = copies((cols_in,), (cols,), small)

    def fetch(b):
        return pltpu.make_async_copy(remote.at[b], held.at[b], sems.at[b])

    for b in range(rows):
        fetch(b).start()
    wait_side = copies((side_in,), (side,), sems.at[pl.ds(rows, 1)])
    wait()
    device = cols[0, 0] // rows

    def some(step, carry):
        b = step * len(sums)
        for n in range(len(sums)):
            fetch(b + n).wait()
        collapse_rows(cols, b, rows, device, held, sums)
        for n, part in enumerate(sums):
            put_halves(matrix, lanes_of(b + n), [pair_of(part, 2 * c) for c in range(rows)])
        return carry

    lax.fori_loop(0, rows // len(sums), some, 0)
    wait_side()
    own = pack(side)
    first[...] = own
    product[...] = apply_t(own, matrix[:, : 2 * rows * N])


def collapse_out(cols, blocks, put, sums):
    rows = blocks.shape[0]
    device = cols[0, 0] // rows
    sums = [part.at[: 2 * rows] for part in sums]

    def some(step, carry):
        b = step * len(sums)
        collapse_rows(cols, b, rows, device, blocks, sums)
        for n, part in enumerate(sums):
            for c in range(rows):
                put(b + n, c, pair_of(part, 2 * c))
        return carry

    lax.fori_loop(0, rows // len(sums), some, 0)


def prepare_mid(cols_in, agg_in, blocks, prolong, direction, matrix, product, send, small, cols, agg, *sums):
    wait = copies((cols_in, agg_in), (cols, agg), small)
    own_product(direction, matrix, product)
    rows = blocks.shape[0]
    half = rows // 2
    n_mid = rows * N
    at = rows * n_mid
    for p in range(half):
        send[at + p * N : at + (p + 1) * N] = jnp.concatenate([prolong[2 * p], prolong[2 * p + 1]], axis=1)
    at += half * N
    wait()

    def put(b, c, value):
        send[pl.ds(pl.multiple_of(c * n_mid + b * N, N), N)] = value

    collapse_out(cols, blocks, put, sums)
    device = cols[0, 0] // rows
    row = lax.broadcasted_iota(jnp.int32, (8, 2 * N), 0)
    joined = jnp.zeros((8, 2 * N), jnp.int32)
    for b in range(rows):
        joined = jnp.where(row == b, local(agg[b], half, device), joined)
    send[at : at + 8] = joined.astype(F32)


def prepare_low(
    cols_in, cols_top_in, agg_in, blocks, prolong, direction, matrix, product, send, transfer, small, cols, cols_top, agg, *sums
):
    wait = copies((cols_in, cols_top_in, agg_in), (cols, cols_top, agg), small)
    own_product(direction, matrix, product)
    n_low = blocks.shape[0] * N
    wait()

    def put(b, c, value):
        send[pl.ds(pl.multiple_of(c * n_low + b * N, N), N)] = value

    collapse_out(cols, blocks, put, sums)
    rows = prolong.shape[0]
    device = cols_top[0, 0] // rows
    for b in range(rows):
        at = local(agg[b], rows // 2, device)
        put_halves(transfer, slice(b * N, (b + 1) * N), spread(at, rows // 2, prolong[b]))


def own_product(vector, matrix, product):
    product[...] = apply_t(vector[...], matrix[:, : matrix.shape[1] // 2])


def other_product(product, other, matrix):
    return product[...] + apply_t(other, matrix[:, matrix.shape[1] // 2 :])


def step_first(first, product, other, matrix, direction, residual):
    d = first[...]
    r = d - (d + other_product(product, pack(other), matrix))
    residual[...] = r
    direction[...] = W[0][0] * d + W[0][1] * r


def step_second(first, old, residual, product, other, matrix, direction, new_residual, total):
    d = old[...]
    r = residual[...] - (d + other_product(product, other[...], matrix))
    new_residual[...] = r
    new = W[1][0] * d + W[1][1] * r
    direction[...] = new
    total[...] = first[...] + d + new


def step_third(old, residual, product, other, matrix, transfer, new_residual, other_part):
    r = residual[...] - (old[...] + other_product(product, other[...], matrix))
    new_residual[...] = r
    other_part[...] = apply_n(r, transfer[:, transfer.shape[1] // 2 :])


def restrict_own(residual, transfer_top, source, own_part, out, matrix, transfer):
    r = residual[...]
    own_part[...] = apply_n(r, transfer_top[:, : transfer_top.shape[1] // 2])
    unpack(r, out)
    join_mid(source, matrix, transfer, False)


def add_mid(a, b, after, out):
    out[...] = a[...] + b[...]


def own_mid(side, matrix, low, product, low_out):
    product[...] = apply_t(side[...], matrix[:, : matrix.shape[1] // 2])


def join_mid(source, matrix, transfer, turn):
    n_mid = matrix.shape[0]
    rows = n_mid // N
    half = rows // 2
    for c in range(rows):
        to = (c + half) % rows if turn else c
        high, low = split(source[c * n_mid : (c + 1) * n_mid])
        base = (to // half) * 2 * n_mid + (to % half) * 2 * N
        matrix[:, base : base + 2 * N] = high
        matrix[:, base + n_mid : base + n_mid + 2 * N] = low
    at = rows * n_mid
    joined = at + half * N
    for b in range(rows):
        both = source[at + (b // 2) * N : at + (b // 2 + 1) * N]
        block = both[:, (b % 2) * N : (b % 2 + 1) * N]
        to = source[joined + b : joined + b + 1].astype(jnp.int32)
        pieces = spread(to, half, block)
        for p, piece in enumerate(pieces):
            put = (p + half // 2) % half if turn else p
            high, low = split(piece)
            matrix_rows = slice(b * N, (b + 1) * N)
            transfer[matrix_rows, put * 2 * N : (put + 1) * 2 * N] = high
            transfer[matrix_rows, n_mid + put * 2 * N : n_mid + (put + 1) * 2 * N] = low


def join_other(source, side, own, matrix, transfer, product):
    join_mid(source, matrix, transfer, True)
    product[...] = jnp.concatenate([own[...], apply_t(side[...], matrix[:, : matrix.shape[1] // 2])], axis=1)


def multiply(a, b):
    (a_high, a_low), (b_high, b_low) = a, b
    out = jnp.dot(a_high, b_high, preferred_element_type=F32)
    out += jnp.dot(a_high, b_low, preferred_element_type=F32)
    return out + jnp.dot(a_low, b_high, preferred_element_type=F32)


def compose_low(own, other, out):
    half = own.shape[0] // 2
    top = jnp.concatenate([own[:half], own[half:]], axis=1)
    low = jnp.concatenate([other[half:], other[:half]], axis=1)
    pair = jnp.concatenate([top, low], axis=0)
    (a0, b0), (a1, b1) = W[0], W[1]
    square = multiply(split(top), split(pair))
    row = lax.broadcasted_iota(jnp.int32, top.shape, 0)
    column = lax.broadcasted_iota(jnp.int32, top.shape, 1)
    value = jnp.where(row == column, 1.0 + (1.0 + a1 - b1) * a0, 0.0)
    value += (b1 * (b0 - 1.0 - a0) - (1.0 + a1) * b0) * top + (b1 * b0) * square
    out[:half] = value[:, :half]
    out[half:] = value[:, half:]


def compose_fixed(own, other, transfer, pair, fine, partial, matrix):
    half = own.shape[0] // 2
    width = 2 * half
    near, far = [], []
    for at, source in ((0, own), (1, other)):
        solve = jnp.concatenate([source[:half], source[half:]], axis=1)
        here = transfer[:, at * half : (at + 1) * half], transfer[:, width + at * half : width + (at + 1) * half]
        product = multiply(here, split(solve))
        near.append(product[:, :half])
        far.append(product[:, half:])
    partial[...] = fine[...] + apply_t(pair[...], jnp.concatenate(split(jnp.concatenate(near, axis=1)), axis=1))
    high, low = split(jnp.concatenate(far, axis=1))
    matrix[:, :width] = high
    matrix[:, width:] = low


def solve_mid(product, own, other, matrix_own, matrix_other, transfer_own, transfer_other, low_pair, solution):
    half = own.shape[1]
    mid = matrix_own.shape[1] // 2

    def pair_product(value, columns):
        return jnp.concatenate(
            [apply_t(value, matrix_own[:, columns]), apply_t(value, matrix_other[:, columns])], axis=1
        )

    d = jnp.concatenate([own[...], other[...]], axis=1)
    r = d - (d + product[...] + pair_product(other[...], slice(mid, 2 * mid)))
    x = d[:, :half]
    for step in range(2):
        d = W[step][0] * d + W[step][1] * r
        x = x + d[:, :half]
        r = r - (d + pair_product(d[:, :half], slice(0, mid)) + pair_product(d[:, half:], slice(mid, 2 * mid)))
    solution[...] = x
    low_pair[...] = apply_n(r[:, :half], transfer_own[...]) + apply_n(r[:, half:], transfer_other[...])


def end_fixed(partial, other, matrix, fixed):
    fixed[...] = partial[...] + apply_t(other[...], matrix[...])


def start_correction(total, fixed, transfer, out):
    out[...] = total[...] + apply_t(fixed[...], transfer[:, : transfer.shape[1] // 2])


def end_correction(partial, other, transfer, out):
    unpack(other_product(partial, other[...], transfer), out)


def per_device(
    flips,
    right_side,
    operator_top,
    columns_top,
    aggregate_top,
    prolong_top,
    operator_mid,
    columns_mid,
    aggregate_mid,
    prolong_mid,
    operator_low,
    columns_low,
):
    def flip(value, level):
        return lax.ppermute(value, ("gx", "gy"), flips[level])

    rows = operator_top.shape[0]
    n_top = rows * N
    n_mid = n_top // 2
    n_low = n_mid // 2
    vec_top = ((S, n_top), F32)
    vec_mid = ((S, n_mid), F32)
    sums = [pltpu.VMEM((2 * rows, N, N), F32)] * 2
    mid_pieces = ((rows // 2 * n_mid + rows // 4 * N + 8, 2 * N), F32)
    low_pieces = ((rows // 4 * n_low, 2 * N), F32)

    other = flip(right_side, 0)
    matrix, first, product = call(
        "prepare_top",
        prepare_top,
        [((n_top, 4 * n_top), BF16), vec_top, vec_top],
        columns_top,
        right_side,
        operator_top,
        remote=range(3),
        scratch=[
            pltpu.SemaphoreType.DMA((1,)),
            pltpu.SMEM(columns_top.shape, jnp.int32),
            pltpu.VMEM(right_side.shape, F32),
            pltpu.VMEM(operator_top.shape, F32),
            pltpu.SemaphoreType.DMA((rows + 1,)),
        ]
        + sums,
        limit=14,
    )
    d1, r1 = call("step_first", step_first, [vec_top, vec_top], first, product, other, matrix)
    other = flip(d1, 0)
    product, send_mid = call(
        "prepare_mid",
        prepare_mid,
        [vec_top, mid_pieces],
        columns_mid,
        aggregate_mid,
        operator_mid,
        prolong_mid,
        d1,
        matrix,
        scratch=index_scratch(columns_mid, aggregate_mid) + sums,
    )
    mid_arrived = flip(send_mid, 1)
    d2, r2, total = call("step_second", step_second, [vec_top] * 3, first, d1, r1, product, other, matrix)
    other = flip(d2, 0)
    product, send_low, transfer = call(
        "prepare_low",
        prepare_low,
        [vec_top, low_pieces, ((n_top, 4 * n_mid), BF16)],
        columns_low,
        columns_top,
        aggregate_top,
        operator_low,
        prolong_top,
        d2,
        matrix,
        scratch=index_scratch(columns_low, columns_top, aggregate_top) + sums,
    )
    low_arrived = flip(send_low, 2)
    smoothed, other_part = call("step_third", step_third, [vec_top, vec_mid], d2, r2, product, other, matrix, transfer)
    arrived = flip(other_part, 0)
    own_part, smoothed_blocks, mid_own, transfer_own = call(
        "restrict_own",
        restrict_own,
        [vec_mid, ((rows, S, N), F32), ((n_mid, 4 * n_mid), BF16), ((n_mid, 4 * n_low), BF16)],
        smoothed,
        transfer,
        send_mid,
    )
    (solve_own,) = call("compose_low", compose_low, [low_pieces], send_low, low_arrived)
    (mid_side,) = call("add_mid", add_mid, [vec_mid], own_part, arrived, solve_own)
    other = flip(mid_side, 1)
    product, solve_own = call("own_mid", own_mid, [vec_mid, low_pieces], mid_side, mid_own, solve_own, aliases={2: 1})
    solve_other = flip(solve_own, 1)
    mid_other, transfer_other, product = call(
        "join_other",
        join_other,
        [((n_mid, 4 * n_mid), BF16), ((n_mid, 4 * n_low), BF16), vec_top],
        mid_arrived,
        mid_side,
        product,
    )
    low_pair, x_mid = call(
        "solve_mid",
        solve_mid,
        [((S, 2 * n_low), F32), vec_mid],
        product,
        mid_side,
        other,
        mid_own,
        mid_other,
        transfer_own,
        transfer_other,
    )
    other = flip(low_pair, 2)
    partial, fixing = call(
        "compose_fixed",
        compose_fixed,
        [vec_mid, ((n_mid, 4 * n_low), BF16)],
        solve_own,
        solve_other,
        transfer_own,
        low_pair,
        x_mid,
    )
    (mid_fixed,) = call("end_fixed", end_fixed, [vec_mid], partial, other, fixing)
    other = flip(mid_fixed, 0)
    (partial,) = call("start_correction", start_correction, [vec_top], total, mid_fixed, transfer)
    (correction,) = call("end_correction", end_correction, [((rows, S, N), F32)], partial, other, transfer)
    return correction, smoothed_blocks


def solution(mesh):
    n_gx, n_gy = mesh.shape["gx"], mesh.shape["gy"]
    masks = (n_gy // 2, n_gx // 2 * n_gy, n_gy // 4)
    flips = [[(source, source ^ mask) for source in range(n_gx * n_gy)] for mask in masks]
    lead = ("gx", "gy")
    in_specs = (
        P(lead, None, None),
        P(lead, None, None, None),
        P(lead, None),
        P(lead),
        P(lead, None, None),
        P(lead, None, None, None),
        P(lead, None),
        P(lead),
        P(lead, None, None),
        P(lead, None, None, None),
        P(lead, None),
    )
    out_specs = (P(lead, None, None), P(lead, None, None))
    return jax.shard_map(
        functools.partial(per_device, flips), mesh=mesh, in_specs=in_specs, out_specs=out_specs, check_vma=False
    )
```

```python
import functools

import jax
import jax.numpy as jnp
from jax import lax
from jax.experimental import pallas as pl
from jax.experimental.pallas import tpu as pltpu
from jax.sharding import PartitionSpec as P

center = 1.0
half_width = 0.6
F32 = jnp.float32
BF16 = jnp.bfloat16
N = 64
S = 8
J = 27


def chebyshev_weights():
    sigma = center / half_width
    rho = half_width / center
    weights = []
    for step in range(3):
        rho_next = 1.0 / (2.0 * sigma - rho)
        weights.append((rho_next * rho, 2.0 * rho_next / half_width))
        rho = rho_next
    return weights


W = chebyshev_weights()
COST = {"prepare_top": 4000, "step_first": 4000, "step_second": 100000, "step_third": 6000, "solve_mid": 20000}


def call(name, body, outs, *args, remote=(), scalars=(), scratch=(), aliases=None, limit=8):
    spaces = [
        pltpu.HBM if at in remote else pltpu.SMEM if at in scalars else pltpu.VMEM for at in range(len(args))
    ]
    args = [pltpu.with_memory_space_constraint(a, m) for a, m in zip(args, spaces)]
    places = [pltpu.SMEM if dtype == jnp.int32 else pltpu.VMEM for _, dtype in outs]
    return pl.pallas_call(
        body,
        name=name,
        out_shape=[place(shape, dtype) for place, (shape, dtype) in zip(places, outs)],
        in_specs=[pl.BlockSpec(memory_space=m) for m in spaces],
        out_specs=[pl.BlockSpec(memory_space=m) for m in places],
        scratch_shapes=scratch,
        input_output_aliases=aliases or {},
        cost_estimate=pl.CostEstimate(flops=COST.get(name, 200) * 1000000, bytes_accessed=0, transcendentals=0),
        compiler_params=pltpu.CompilerParams(vmem_limit_bytes=limit * 1024 * 1024),
    )(*args)


def copies(sources, targets, sems):
    moves = [pltpu.make_async_copy(s, t, sems.at[n]) for n, (s, t) in enumerate(zip(sources, targets))]
    for move in moves:
        move.start()

    def wait():
        for move in moves:
            move.wait()

    return wait


def split(value):
    high = value.astype(BF16)
    return high, (value - high.astype(F32)).astype(BF16)


def stack(value):
    return jnp.concatenate(split(value), axis=0)


def fold(value):
    return value[:S] + value[S:]


def apply_t(vector, matrix):
    both = stack(vector)
    both = jnp.concatenate([both, both], axis=1)
    out = lax.dot_general(both, matrix, (((1,), (1,)), ((), ())), preferred_element_type=F32)
    return fold(out)


def apply_turned(vector, matrix):
    both = stack(vector)
    both = jnp.concatenate([both, both], axis=1)
    return fold(jnp.dot(both, matrix, preferred_element_type=F32))


def apply_n(vector, matrix):
    out = fold(lax.dot_general(stack(vector), matrix, (((1,), (0,)), ((), ())), preferred_element_type=F32))
    half = out.shape[1] // 2
    return out[:, :half] + out[:, half:]


def pack(ref):
    return jnp.concatenate([ref[b] for b in range(ref.shape[0])], axis=1)


def unpack(value, ref):
    for b in range(ref.shape[0]):
        ref[b] = value[:, b * N : (b + 1) * N]


def local(index, rows, device):
    offset = index ^ (device * rows)
    return jnp.minimum(offset, rows + (offset & (rows - 1)))


def collapse_rows(cols, b, rows, device, blocks, sums):
    for part in sums:
        part[...] = jnp.zeros(part.shape, F32)
    for j in range(J):
        for n, part in enumerate(sums):
            at = local(cols[b + n, j], rows, device)
            part[at] = part[at] + blocks[b + n, j]


def pair_of(sums, at):
    return jnp.concatenate([sums[at], sums[at + 1]], axis=1)


def spread(at, rows, block):
    twice = jnp.concatenate([block, block], axis=1)
    lane = lax.broadcasted_iota(jnp.int32, (N, 2 * N), 1) // N
    return [jnp.where(lane + 2 * piece == at, twice, 0.0) for piece in range(rows)]


def put_halves(ref, rows_at, pieces):
    half = len(pieces) // 2
    width = half * 2 * N
    for p, piece in enumerate(pieces):
        high, low = split(piece)
        base = (p // half) * 2 * width + (p % half) * 2 * N
        ref[rows_at, pl.ds(base, 2 * N)] = high
        ref[rows_at, pl.ds(base + width, 2 * N)] = low


def lanes_of(b):
    return pl.ds(pl.multiple_of(b * N, N), N)


def prepare_top(
    cols_in, side_in, remote, agg_in, cols_mid_in, agg_mid_in, cols_low_in,
    matrix, first, product, agg, cols_mid, agg_mid, cols_low,
    small, cols, side, held, sems, *sums
):
    rows = remote.shape[0]
    wait = copies((cols_in,), (cols,), small)

    def fetch(b):
        return pltpu.make_async_copy(remote.at[b], held.at[b], sems.at[b])

    for b in range(rows):
        fetch(b).start()
    wait_more = copies(
        (side_in, agg_in, cols_mid_in, agg_mid_in, cols_low_in),
        (side, agg, cols_mid, agg_mid, cols_low),
        sems.at[pl.ds(rows, 5)],
    )
    wait()
    device = cols[0, 0] // rows

    def some(step, carry):
        b = step * len(sums)
        for n in range(len(sums)):
            fetch(b + n).wait()
        collapse_rows(cols, b, rows, device, held, sums)
        for n, part in enumerate(sums):
            put_halves(matrix, lanes_of(b + n), [pair_of(part, 2 * c) for c in range(rows)])
        return carry

    lax.fori_loop(0, rows // len(sums), some, 0)
    wait_more()
    own = pack(side)
    first[...] = own
    product[...] = apply_t(own, matrix[:, : 2 * rows * N])


def collapse_out(cols, blocks, put, sums):
    rows = blocks.shape[0]
    device = cols[0, 0] // rows
    sums = [part.at[: 2 * rows] for part in sums]

    def some(step, carry):
        b = step * len(sums)
        collapse_rows(cols, b, rows, device, blocks, sums)
        for n, part in enumerate(sums):
            for c in range(rows):
                put(b + n, c, pair_of(part, 2 * c))
        return carry

    lax.fori_loop(0, rows // len(sums), some, 0)


def prepare_mid(cols, agg, blocks, prolong, after, send, *sums):
    rows = blocks.shape[0]
    half = rows // 2
    n_mid = rows * N

    def put(b, c, value):
        send[pl.ds(pl.multiple_of(c * n_mid + b * N, N), N)] = value

    collapse_out(cols, blocks, put, sums)
    at = rows * n_mid
    for p in range(half):
        send[at + p * N : at + (p + 1) * N] = jnp.concatenate([prolong[2 * p], prolong[2 * p + 1]], axis=1)
    at += half * N
    device = cols[0, 0] // rows
    row = lax.broadcasted_iota(jnp.int32, (8, 2 * N), 0)
    joined = jnp.zeros((8, 2 * N), jnp.int32)
    for b in range(rows):
        joined = jnp.where(row == b, local(agg[b], half, device), joined)
    send[at : at + 8] = joined.astype(F32)


def prepare_low(
    cols, agg, blocks, prolong, direction, residual, matrix, send, transfer, turned, known, part, restrict, *sums
):
    turned[...] = matrix[:, matrix.shape[1] // 2 :].T
    known[...] = residual[...] - (direction[...] + apply_t(direction[...], matrix[:, : matrix.shape[1] // 2]))
    n_low = blocks.shape[0] * N

    def put(b, c, value):
        send[pl.ds(pl.multiple_of(c * n_low + b * N, N), N)] = value

    collapse_out(cols, blocks, put, sums)
    rows = prolong.shape[0]
    device = cols[0, 0] // blocks.shape[0]
    for b in range(rows):
        at = local(agg[b], rows // 2, device)
        put_halves(transfer, slice(b * N, (b + 1) * N), spread(at, rows // 2, prolong[b]))
    half = transfer.shape[1] // 2
    part[...] = apply_n(known[...], transfer[:, half:])
    depth = turned.shape[0] // 2
    high, low = split(
        multiply(
            (turned[:depth], turned[depth:]), (transfer[:, half : half + half // 2], transfer[:, half + half // 2 :])
        )
    )
    restrict[:depth] = high
    restrict[depth:] = low


def own_product(vector, matrix, after, product):
    product[...] = apply_t(vector[...], matrix[:, : matrix.shape[1] // 2])


def other_product(product, other, matrix):
    return product[...] + apply_t(other, matrix[:, matrix.shape[1] // 2 :])


def step_first(first, product, other, matrix, direction, residual):
    d = first[...]
    r = d - (d + other_product(product, pack(other), matrix))
    residual[...] = r
    direction[...] = W[0][0] * d + W[0][1] * r


def step_second(first, old, residual, product, other, matrix, direction, new_residual, total):
    d = old[...]
    r = residual[...] - (d + other_product(product, other[...], matrix))
    new_residual[...] = r
    new = W[1][0] * d + W[1][1] * r
    direction[...] = new
    total[...] = first[...] + d + new


def step_third(part, other, restrict, other_part):
    other_part[...] = part[...] - apply_turned(other[...], restrict[...])


def restrict_own(known, other, turned, transfer_top, source, own_part, out, matrix, transfer):
    r = known[...] - apply_turned(other[...], turned[...])
    own_part[...] = apply_n(r, transfer_top[:, : transfer_top.shape[1] // 2])
    unpack(r, out)
    join_mid(source, matrix, transfer, False)


def add_mid(a, b, after, out):
    out[...] = a[...] + b[...]


def own_mid(side, matrix, low, product, low_out):
    product[...] = apply_turned(side[...], matrix[: matrix.shape[0] // 2])


def join_mid(source, matrix, transfer, turn):
    n_mid = matrix.shape[1]
    rows = n_mid // N
    half = rows // 2
    for c in range(rows):
        to = (c + half) % rows if turn else c
        high, low = split(source[c * n_mid : (c + 1) * n_mid].T)
        base = (to // half) * 2 * n_mid + (to % half) * 2 * N
        matrix[base : base + 2 * N] = high
        matrix[base + n_mid : base + n_mid + 2 * N] = low
    at = rows * n_mid
    joined = at + half * N
    for b in range(rows):
        both = source[at + (b // 2) * N : at + (b // 2 + 1) * N]
        block = both[:, (b % 2) * N : (b % 2 + 1) * N]
        to = source[joined + b : joined + b + 1].astype(jnp.int32)
        pieces = spread(to, half, block)
        for p, piece in enumerate(pieces):
            put = (p + half // 2) % half if turn else p
            high, low = split(piece)
            matrix_rows = slice(b * N, (b + 1) * N)
            transfer[matrix_rows, put * 2 * N : (put + 1) * 2 * N] = high
            transfer[matrix_rows, n_mid + put * 2 * N : n_mid + (put + 1) * 2 * N] = low


def join_other(source, side, own, matrix, transfer, product):
    join_mid(source, matrix, transfer, True)
    other = apply_turned(side[...], matrix[: matrix.shape[0] // 2])
    product[...] = jnp.concatenate([own[...], other], axis=1)


def multiply(a, b):
    (a_high, a_low), (b_high, b_low) = a, b
    out = jnp.dot(a_high, b_high, preferred_element_type=F32)
    out += jnp.dot(a_high, b_low, preferred_element_type=F32)
    return out + jnp.dot(a_low, b_high, preferred_element_type=F32)


def compose_low(own, other, out):
    half = own.shape[0] // 2
    top = jnp.concatenate([own[:half], own[half:]], axis=1)
    low = jnp.concatenate([other[half:], other[:half]], axis=1)
    pair = jnp.concatenate([top, low], axis=0)
    (a0, b0), (a1, b1) = W[0], W[1]
    square = multiply(split(top), split(pair))
    row = lax.broadcasted_iota(jnp.int32, top.shape, 0)
    column = lax.broadcasted_iota(jnp.int32, top.shape, 1)
    value = jnp.where(row == column, 1.0 + (1.0 + a1 - b1) * a0, 0.0)
    value += (b1 * (b0 - 1.0 - a0) - (1.0 + a1) * b0) * top + (b1 * b0) * square
    out[:half] = value[:, :half]
    out[half:] = value[:, half:]


def compose_fixed(own, other, transfer, pair, fine, partial, matrix):
    half = own.shape[0] // 2
    width = 2 * half
    near, far = [], []
    for at, source in ((0, own), (1, other)):
        solve = jnp.concatenate([source[:half], source[half:]], axis=1)
        here = transfer[:, at * half : (at + 1) * half], transfer[:, width + at * half : width + (at + 1) * half]
        product = multiply(here, split(solve))
        near.append(product[:, :half])
        far.append(product[:, half:])
    partial[...] = fine[...] + apply_t(pair[...], jnp.concatenate(split(jnp.concatenate(near, axis=1)), axis=1))
    high, low = split(jnp.concatenate(far, axis=1).T)
    matrix[:width] = high
    matrix[width:] = low


def solve_mid(product, own, other, matrix_own, matrix_other, transfer_own, transfer_other, low_pair, solution):
    half = own.shape[1]
    mid = matrix_own.shape[0] // 2

    def pair_product(value, columns):
        return jnp.concatenate(
            [apply_turned(value, matrix_own[columns]), apply_turned(value, matrix_other[columns])], axis=1
        )

    d = jnp.concatenate([own[...], other[...]], axis=1)
    r = d - (d + product[...] + pair_product(other[...], slice(mid, 2 * mid)))
    x = d[:, :half]
    for step in range(2):
        d = W[step][0] * d + W[step][1] * r
        x = x + d[:, :half]
        r = r - (d + pair_product(d[:, :half], slice(0, mid)) + pair_product(d[:, half:], slice(mid, 2 * mid)))
    solution[...] = x
    low_pair[...] = apply_n(r[:, :half], transfer_own[...]) + apply_n(r[:, half:], transfer_other[...])


def end_fixed(partial, other, matrix, fixed):
    fixed[...] = partial[...] + apply_turned(other[...], matrix[...])


def start_correction(total, fixed, transfer, out, turned):
    half = transfer.shape[1] // 2
    turned[...] = transfer[:, half:].T
    out[...] = total[...] + apply_t(fixed[...], transfer[:, :half])


def end_correction(partial, other, turned, out):
    unpack(partial[...] + apply_turned(other[...], turned[...]), out)


def per_device(
    flips,
    right_side,
    operator_top,
    columns_top,
    aggregate_top,
    prolong_top,
    operator_mid,
    columns_mid,
    aggregate_mid,
    prolong_mid,
    operator_low,
    columns_low,
):
    def flip(value, level):
        return lax.ppermute(value, ("gx", "gy"), flips[level])

    rows = operator_top.shape[0]
    n_top = rows * N
    n_mid = n_top // 2
    n_low = n_mid // 2
    vec_top = ((S, n_top), F32)
    vec_mid = ((S, n_mid), F32)
    sums = [pltpu.VMEM((2 * rows, N, N), F32)] * 2
    mid_pieces = ((rows // 2 * n_mid + rows // 4 * N + 8, 2 * N), F32)
    low_pieces = ((rows // 4 * n_low, 2 * N), F32)

    other = flip(right_side, 0)
    indices = (aggregate_top, columns_mid, aggregate_mid, columns_low)
    matrix, first, product, agg_top, cols_mid, agg_mid, cols_low = call(
        "prepare_top",
        prepare_top,
        [((n_top, 4 * n_top), BF16), vec_top, vec_top] + [(a.shape, jnp.int32) for a in indices],
        columns_top,
        right_side,
        operator_top,
        *indices,
        remote=range(7),
        scratch=[
            pltpu.SemaphoreType.DMA((1,)),
            pltpu.SMEM(columns_top.shape, jnp.int32),
            pltpu.VMEM(right_side.shape, F32),
            pltpu.VMEM(operator_top.shape, F32),
            pltpu.SemaphoreType.DMA((rows + 5,)),
        ]
        + sums,
        limit=14,
    )
    d1, r1 = call("step_first", step_first, [vec_top, vec_top], first, product, other, matrix)
    other = flip(d1, 0)
    (send_mid,) = call(
        "prepare_mid",
        prepare_mid,
        [mid_pieces],
        cols_mid,
        agg_mid,
        operator_mid,
        prolong_mid,
        d1,
        scalars=(0, 1),
        scratch=sums,
    )
    mid_arrived = flip(send_mid, 1)
    (product,) = call("own_top", own_product, [vec_top], d1, matrix, send_mid)
    d2, r2, total = call("step_second", step_second, [vec_top] * 3, first, d1, r1, product, other, matrix)
    other = flip(d2, 0)
    send_low, transfer, turned, known, part, restrict = call(
        "prepare_low",
        prepare_low,
        [low_pieces, ((n_top, 4 * n_mid), BF16), ((2 * n_top, n_top), BF16), vec_top, vec_mid, ((2 * n_top, n_mid), BF16)],
        cols_low,
        agg_top,
        operator_low,
        prolong_top,
        d2,
        r2,
        matrix,
        scalars=(0, 1),
        scratch=sums,
    )
    low_arrived = flip(send_low, 2)
    (other_part,) = call("step_third", step_third, [vec_mid], part, other, restrict)
    arrived = flip(other_part, 0)
    own_part, smoothed_blocks, mid_own, transfer_own = call(
        "restrict_own",
        restrict_own,
        [vec_mid, ((rows, S, N), F32), ((4 * n_mid, n_mid), BF16), ((n_mid, 4 * n_low), BF16)],
        known,
        other,
        turned,
        transfer,
        send_mid,
    )
    (solve_own,) = call("compose_low", compose_low, [low_pieces], send_low, low_arrived)
    (mid_side,) = call("add_mid", add_mid, [vec_mid], own_part, arrived, solve_own)
    other = flip(mid_side, 1)
    product, solve_own = call("own_mid", own_mid, [vec_mid, low_pieces], mid_side, mid_own, solve_own, aliases={2: 1})
    solve_other = flip(solve_own, 1)
    mid_other, transfer_other, product = call(
        "join_other",
        join_other,
        [((4 * n_mid, n_mid), BF16), ((n_mid, 4 * n_low), BF16), vec_top],
        mid_arrived,
        mid_side,
        product,
    )
    low_pair, x_mid = call(
        "solve_mid",
        solve_mid,
        [((S, 2 * n_low), F32), vec_mid],
        product,
        mid_side,
        other,
        mid_own,
        mid_other,
        transfer_own,
        transfer_other,
    )
    other = flip(low_pair, 2)
    partial, fixing = call(
        "compose_fixed",
        compose_fixed,
        [vec_mid, ((4 * n_low, n_mid), BF16)],
        solve_own,
        solve_other,
        transfer_own,
        low_pair,
        x_mid,
    )
    (mid_fixed,) = call("end_fixed", end_fixed, [vec_mid], partial, other, fixing)
    other = flip(mid_fixed, 0)
    partial, turned = call(
        "start_correction", start_correction, [vec_top, ((2 * n_mid, n_top), BF16)], total, mid_fixed, transfer
    )
    (correction,) = call("end_correction", end_correction, [((rows, S, N), F32)], partial, other, turned)
    return correction, smoothed_blocks


def solution(mesh):
    n_gx, n_gy = mesh.shape["gx"], mesh.shape["gy"]
    masks = (n_gy // 2, n_gx // 2 * n_gy, n_gy // 4)
    flips = [[(source, source ^ mask) for source in range(n_gx * n_gy)] for mask in masks]
    lead = ("gx", "gy")
    in_specs = (
        P(lead, None, None),
        P(lead, None, None, None),
        P(lead, None),
        P(lead),
        P(lead, None, None),
        P(lead, None, None, None),
        P(lead, None),
        P(lead),
        P(lead, None, None),
        P(lead, None, None, None),
        P(lead, None),
    )
    out_specs = (P(lead, None, None), P(lead, None, None))
    return jax.shard_map(
        functools.partial(per_device, flips), mesh=mesh, in_specs=in_specs, out_specs=out_specs, check_vma=False
    )
```

```python
import functools

import jax
import jax.numpy as jnp
from jax import lax
from jax.experimental import pallas as pl
from jax.experimental.pallas import tpu as pltpu
from jax.sharding import PartitionSpec as P

center = 1.0
half_width = 0.6
F32 = jnp.float32
BF16 = jnp.bfloat16
N = 64
S = 8
J = 27


def chebyshev_weights():
    sigma = center / half_width
    rho = half_width / center
    weights = []
    for step in range(3):
        rho_next = 1.0 / (2.0 * sigma - rho)
        weights.append((rho_next * rho, 2.0 * rho_next / half_width))
        rho = rho_next
    return weights


W = chebyshev_weights()
COST = {"prepare_top": 4000, "step_first": 4000, "step_second": 100000, "step_third": 6000, "solve_mid": 20000}


def call(name, body, outs, *args, remote=(), scalars=(), scratch=(), aliases=None, limit=8):
    spaces = [
        pltpu.HBM if at in remote else pltpu.SMEM if at in scalars else pltpu.VMEM for at in range(len(args))
    ]
    args = [pltpu.with_memory_space_constraint(a, m) for a, m in zip(args, spaces)]
    places = [pltpu.SMEM if dtype == jnp.int32 else pltpu.VMEM for _, dtype in outs]
    return pl.pallas_call(
        body,
        name=name,
        out_shape=[place(shape, dtype) for place, (shape, dtype) in zip(places, outs)],
        in_specs=[pl.BlockSpec(memory_space=m) for m in spaces],
        out_specs=[pl.BlockSpec(memory_space=m) for m in places],
        scratch_shapes=scratch,
        input_output_aliases=aliases or {},
        cost_estimate=pl.CostEstimate(flops=COST.get(name, 200) * 1000000, bytes_accessed=0, transcendentals=0),
        compiler_params=pltpu.CompilerParams(vmem_limit_bytes=limit * 1024 * 1024),
    )(*args)


def copies(sources, targets, sems):
    moves = [pltpu.make_async_copy(s, t, sems.at[n]) for n, (s, t) in enumerate(zip(sources, targets))]
    for move in moves:
        move.start()

    def wait():
        for move in moves:
            move.wait()

    return wait


def split(value):
    high = value.astype(BF16)
    return high, (value - high.astype(F32)).astype(BF16)


def stack(value):
    return jnp.concatenate(split(value), axis=0)


def fold(value):
    return value[:S] + value[S:]


def apply_t(vector, matrix):
    both = stack(vector)
    both = jnp.concatenate([both, both], axis=1)
    out = lax.dot_general(both, matrix, (((1,), (1,)), ((), ())), preferred_element_type=F32)
    return fold(out)


def apply_turned(vector, matrix):
    both = stack(vector)
    both = jnp.concatenate([both, both], axis=1)
    return fold(jnp.dot(both, matrix, preferred_element_type=F32))


def apply_n(vector, matrix):
    out = fold(lax.dot_general(stack(vector), matrix, (((1,), (0,)), ((), ())), preferred_element_type=F32))
    half = out.shape[1] // 2
    return out[:, :half] + out[:, half:]


def pack(ref):
    return jnp.concatenate([ref[b] for b in range(ref.shape[0])], axis=1)


def unpack(value, ref):
    for b in range(ref.shape[0]):
        ref[b] = value[:, b * N : (b + 1) * N]


def local(index, rows, device):
    offset = index ^ (device * rows)
    return jnp.minimum(offset, rows + (offset & (rows - 1)))


def collapse_rows(cols, b, rows, device, blocks, sums):
    for part in sums:
        part[...] = jnp.zeros(part.shape, F32)
    for j in range(J):
        for n, part in enumerate(sums):
            at = local(cols[b + n, j], rows, device)
            part[at] = part[at] + blocks[b + n, j]


def pair_of(sums, at):
    return jnp.concatenate([sums[at], sums[at + 1]], axis=1)


def spread(at, rows, block):
    twice = jnp.concatenate([block, block], axis=1)
    lane = lax.broadcasted_iota(jnp.int32, (N, 2 * N), 1) // N
    return [jnp.where(lane + 2 * piece == at, twice, 0.0) for piece in range(rows)]


def put_halves(ref, rows_at, pieces):
    half = len(pieces) // 2
    width = half * 2 * N
    for p, piece in enumerate(pieces):
        high, low = split(piece)
        base = (p // half) * 2 * width + (p % half) * 2 * N
        ref[rows_at, pl.ds(base, 2 * N)] = high
        ref[rows_at, pl.ds(base + width, 2 * N)] = low


def prepare_top(
    cols_in, side_in, remote, agg_in, cols_mid_in, agg_mid_in, cols_low_in,
    matrix, first, product, agg, cols_mid, agg_mid, cols_low,
    small, cols, side, held, sems, *sums
):
    rows = remote.shape[0]
    wait = copies((cols_in,), (cols,), small)
    wait_side = copies((side_in,), (side,), sems.at[pl.ds(rows, 1)])

    def fetch(b):
        return pltpu.make_async_copy(remote.at[b], held.at[b], sems.at[b])

    for b in range(rows):
        fetch(b).start()
    wait_more = copies(
        (agg_in, cols_mid_in, agg_mid_in, cols_low_in), (agg, cols_mid, agg_mid, cols_low), sems.at[pl.ds(rows + 1, 4)]
    )
    wait()
    device = cols[0, 0] // rows
    half = 2 * rows * N
    done = 0
    for b in range(0, rows, 2):
        fetch(b).wait()
        fetch(b + 1).wait()
        parts = sums[b % 4 : b % 4 + 2]
        collapse_rows(cols, b, rows, device, held, parts)
        for n, part in enumerate(parts):
            put_halves(matrix, slice((b + n) * N, (b + n + 1) * N), [pair_of(part, 2 * c) for c in range(rows)])
        if b + 2 == rows // 2:
            wait_side()
            first[...] = pack(side)
        if b + 2 > rows // 2:
            product[:, done : b * N] = apply_t(first[...], matrix[done : b * N, :half])
            done = b * N
    product[:, done:] = apply_t(first[...], matrix[done:, :half])
    wait_more()


def collapse_out(cols, blocks, put, sums):
    rows = blocks.shape[0]
    device = cols[0, 0] // rows
    sums = [part.at[: 2 * rows] for part in sums]
    for b in range(0, rows, 2):
        parts = sums[b % 4 : b % 4 + 2]
        collapse_rows(cols, b, rows, device, blocks, parts)
        for n, part in enumerate(parts):
            for c in range(rows):
                put(b + n, c, pair_of(part, 2 * c))


def prepare_mid(cols, agg, blocks, prolong, direction, matrix, product, send, turned, *sums):
    turned[...] = matrix[:, matrix.shape[1] // 2 :].T
    product[...] = apply_t(direction[...], matrix[:, : matrix.shape[1] // 2])
    rows = blocks.shape[0]
    half = rows // 2
    n_mid = rows * N

    def put(b, c, value):
        send[c * n_mid + b * N : c * n_mid + (b + 1) * N] = value

    collapse_out(cols, blocks, put, sums)
    at = rows * n_mid
    for p in range(half):
        send[at + p * N : at + (p + 1) * N] = jnp.concatenate([prolong[2 * p], prolong[2 * p + 1]], axis=1)
    at += half * N
    device = cols[0, 0] // rows
    row = lax.broadcasted_iota(jnp.int32, (8, 2 * N), 0)
    joined = jnp.zeros((8, 2 * N), jnp.int32)
    for b in range(rows):
        joined = jnp.where(row == b, local(agg[b], half, device), joined)
    send[at : at + 8] = joined.astype(F32)


def prepare_low(
    cols, agg, blocks, prolong, direction, residual, matrix, turned, send, transfer, known, part, restrict, *sums
):
    known[...] = residual[...] - (direction[...] + apply_t(direction[...], matrix[:, : matrix.shape[1] // 2]))
    n_low = blocks.shape[0] * N

    def put(b, c, value):
        send[c * n_low + b * N : c * n_low + (b + 1) * N] = value

    collapse_out(cols, blocks, put, sums)
    rows = prolong.shape[0]
    device = cols[0, 0] // blocks.shape[0]
    for b in range(rows):
        at = local(agg[b], rows // 2, device)
        put_halves(transfer, slice(b * N, (b + 1) * N), spread(at, rows // 2, prolong[b]))
    half = transfer.shape[1] // 2
    part[...] = apply_n(known[...], transfer[:, half:])
    depth = turned.shape[0] // 2
    high, low = split(
        multiply(
            (turned[:depth], turned[depth:]), (transfer[:, half : half + half // 2], transfer[:, half + half // 2 :])
        )
    )
    restrict[:depth] = high
    restrict[depth:] = low


def other_product(product, other, matrix):
    return product[...] + apply_t(other, matrix[:, matrix.shape[1] // 2 :])


def step_first(first, product, other, matrix, direction, residual):
    d = first[...]
    r = d - (d + other_product(product, pack(other), matrix))
    residual[...] = r
    direction[...] = W[0][0] * d + W[0][1] * r


def step_second(first, old, residual, product, other, turned, direction, new_residual, total):
    d = old[...]
    r = residual[...] - (d + product[...] + apply_turned(other[...], turned[...]))
    new_residual[...] = r
    new = W[1][0] * d + W[1][1] * r
    direction[...] = new
    total[...] = first[...] + d + new


def step_third(part, other, restrict, other_part):
    other_part[...] = part[...] - apply_turned(other[...], restrict[...])


def restrict_own(known, other, turned, transfer_top, source, own_part, out, matrix, transfer):
    r = known[...] - apply_turned(other[...], turned[...])
    own_part[...] = apply_n(r, transfer_top[:, : transfer_top.shape[1] // 2])
    unpack(r, out)
    join_mid(source, matrix, transfer, False)


def add_mid(a, b, after, out):
    out[...] = a[...] + b[...]


def own_mid(side, matrix, low, product, low_out):
    product[...] = apply_turned(side[...], matrix[: matrix.shape[0] // 2])


def join_mid(source, matrix, transfer, turn):
    n_mid = matrix.shape[1]
    rows = n_mid // N
    half = rows // 2
    for c in range(rows):
        to = (c + half) % rows if turn else c
        high, low = split(source[c * n_mid : (c + 1) * n_mid].T)
        base = (to // half) * 2 * n_mid + (to % half) * 2 * N
        matrix[base : base + 2 * N] = high
        matrix[base + n_mid : base + n_mid + 2 * N] = low
    at = rows * n_mid
    joined = at + half * N
    for b in range(rows):
        both = source[at + (b // 2) * N : at + (b // 2 + 1) * N]
        block = both[:, (b % 2) * N : (b % 2 + 1) * N]
        to = source[joined + b : joined + b + 1].astype(jnp.int32)
        pieces = spread(to, half, block)
        for p, piece in enumerate(pieces):
            put = (p + half // 2) % half if turn else p
            high, low = split(piece)
            matrix_rows = slice(b * N, (b + 1) * N)
            transfer[matrix_rows, put * 2 * N : (put + 1) * 2 * N] = high
            transfer[matrix_rows, n_mid + put * 2 * N : n_mid + (put + 1) * 2 * N] = low


def join_other(source, side, own, matrix, transfer, product):
    join_mid(source, matrix, transfer, True)
    other = apply_turned(side[...], matrix[: matrix.shape[0] // 2])
    product[...] = jnp.concatenate([own[...], other], axis=1)


def multiply(a, b):
    (a_high, a_low), (b_high, b_low) = a, b
    out = jnp.dot(a_high, b_high, preferred_element_type=F32)
    out += jnp.dot(a_high, b_low, preferred_element_type=F32)
    return out + jnp.dot(a_low, b_high, preferred_element_type=F32)


def compose_low(own, other, out):
    half = own.shape[0] // 2
    top = jnp.concatenate([own[:half], own[half:]], axis=1)
    low = jnp.concatenate([other[half:], other[:half]], axis=1)
    pair = jnp.concatenate([top, low], axis=0)
    (a0, b0), (a1, b1) = W[0], W[1]
    square = multiply(split(top), split(pair))
    row = lax.broadcasted_iota(jnp.int32, top.shape, 0)
    column = lax.broadcasted_iota(jnp.int32, top.shape, 1)
    value = jnp.where(row == column, 1.0 + (1.0 + a1 - b1) * a0, 0.0)
    value += (b1 * (b0 - 1.0 - a0) - (1.0 + a1) * b0) * top + (b1 * b0) * square
    out[:half] = value[:, :half]
    out[half:] = value[:, half:]


def compose_fixed(own, other, transfer, pair, fine, partial, matrix):
    half = own.shape[0] // 2
    width = 2 * half
    near, far = [], []
    for at, source in ((0, own), (1, other)):
        solve = jnp.concatenate([source[:half], source[half:]], axis=1)
        here = transfer[:, at * half : (at + 1) * half], transfer[:, width + at * half : width + (at + 1) * half]
        product = multiply(here, split(solve))
        near.append(product[:, :half])
        far.append(product[:, half:])
    partial[...] = fine[...] + apply_t(pair[...], jnp.concatenate(split(jnp.concatenate(near, axis=1)), axis=1))
    high, low = split(jnp.concatenate(far, axis=1).T)
    matrix[:width] = high
    matrix[width:] = low


def solve_mid(product, own, other, matrix_own, matrix_other, transfer_own, transfer_other, low_pair, solution):
    half = own.shape[1]
    mid = matrix_own.shape[0] // 2

    def pair_product(value, columns):
        return jnp.concatenate(
            [apply_turned(value, matrix_own[columns]), apply_turned(value, matrix_other[columns])], axis=1
        )

    d = jnp.concatenate([own[...], other[...]], axis=1)
    r = d - (d + product[...] + pair_product(other[...], slice(mid, 2 * mid)))
    x = d[:, :half]
    for step in range(2):
        d = W[step][0] * d + W[step][1] * r
        x = x + d[:, :half]
        r = r - (d + pair_product(d[:, :half], slice(0, mid)) + pair_product(d[:, half:], slice(mid, 2 * mid)))
    solution[...] = x
    low_pair[...] = apply_n(r[:, :half], transfer_own[...]) + apply_n(r[:, half:], transfer_other[...])


def end_fixed(partial, other, matrix, fixed):
    fixed[...] = partial[...] + apply_turned(other[...], matrix[...])


def start_correction(total, fixed, transfer, out, turned):
    half = transfer.shape[1] // 2
    turned[...] = transfer[:, half:].T
    out[...] = total[...] + apply_t(fixed[...], transfer[:, :half])


def end_correction(partial, other, turned, out):
    unpack(partial[...] + apply_turned(other[...], turned[...]), out)


def per_device(
    flips,
    right_side,
    operator_top,
    columns_top,
    aggregate_top,
    prolong_top,
    operator_mid,
    columns_mid,
    aggregate_mid,
    prolong_mid,
    operator_low,
    columns_low,
):
    def flip(value, level):
        return lax.ppermute(value, ("gx", "gy"), flips[level])

    rows = operator_top.shape[0]
    n_top = rows * N
    n_mid = n_top // 2
    n_low = n_mid // 2
    vec_top = ((S, n_top), F32)
    vec_mid = ((S, n_mid), F32)
    sums = [pltpu.VMEM((2 * rows, N, N), F32)] * 4
    mid_pieces = ((rows // 2 * n_mid + rows // 4 * N + 8, 2 * N), F32)
    low_pieces = ((rows // 4 * n_low, 2 * N), F32)

    other = flip(right_side, 0)
    indices = (aggregate_top, columns_mid, aggregate_mid, columns_low)
    matrix, first, product, agg_top, cols_mid, agg_mid, cols_low = call(
        "prepare_top",
        prepare_top,
        [((n_top, 4 * n_top), BF16), vec_top, vec_top] + [(a.shape, jnp.int32) for a in indices],
        columns_top,
        right_side,
        operator_top,
        *indices,
        remote=range(7),
        scratch=[
            pltpu.SemaphoreType.DMA((1,)),
            pltpu.SMEM(columns_top.shape, jnp.int32),
            pltpu.VMEM(right_side.shape, F32),
            pltpu.VMEM(operator_top.shape, F32),
            pltpu.SemaphoreType.DMA((rows + 5,)),
        ]
        + sums,
        limit=14,
    )
    d1, r1 = call("step_first", step_first, [vec_top, vec_top], first, product, other, matrix)
    other = flip(d1, 0)
    product, send_mid, turned = call(
        "prepare_mid",
        prepare_mid,
        [vec_top, mid_pieces, ((2 * n_top, n_top), BF16)],
        cols_mid,
        agg_mid,
        operator_mid,
        prolong_mid,
        d1,
        matrix,
        scalars=(0, 1),
        scratch=sums,
    )
    mid_arrived = flip(send_mid, 1)
    d2, r2, total = call("step_second", step_second, [vec_top] * 3, first, d1, r1, product, other, turned)
    other = flip(d2, 0)
    send_low, transfer, known, part, restrict = call(
        "prepare_low",
        prepare_low,
        [low_pieces, ((n_top, 4 * n_mid), BF16), vec_top, vec_mid, ((2 * n_top, n_mid), BF16)],
        cols_low,
        agg_top,
        operator_low,
        prolong_top,
        d2,
        r2,
        matrix,
        turned,
        scalars=(0, 1),
        scratch=sums,
    )
    low_arrived = flip(send_low, 2)
    (other_part,) = call("step_third", step_third, [vec_mid], part, other, restrict)
    arrived = flip(other_part, 0)
    own_part, smoothed_blocks, mid_own, transfer_own = call(
        "restrict_own",
        restrict_own,
        [vec_mid, ((rows, S, N), F32), ((4 * n_mid, n_mid), BF16), ((n_mid, 4 * n_low), BF16)],
        known,
        other,
        turned,
        transfer,
        send_mid,
    )
    (solve_own,) = call("compose_low", compose_low, [low_pieces], send_low, low_arrived)
    (mid_side,) = call("add_mid", add_mid, [vec_mid], own_part, arrived, solve_own)
    other = flip(mid_side, 1)
    product, solve_own = call("own_mid", own_mid, [vec_mid, low_pieces], mid_side, mid_own, solve_own, aliases={2: 1})
    solve_other = flip(solve_own, 1)
    mid_other, transfer_other, product = call(
        "join_other",
        join_other,
        [((4 * n_mid, n_mid), BF16), ((n_mid, 4 * n_low), BF16), vec_top],
        mid_arrived,
        mid_side,
        product,
    )
    low_pair, x_mid = call(
        "solve_mid",
        solve_mid,
        [((S, 2 * n_low), F32), vec_mid],
        product,
        mid_side,
        other,
        mid_own,
        mid_other,
        transfer_own,
        transfer_other,
    )
    other = flip(low_pair, 2)
    partial, fixing = call(
        "compose_fixed",
        compose_fixed,
        [vec_mid, ((4 * n_low, n_mid), BF16)],
        solve_own,
        solve_other,
        transfer_own,
        low_pair,
        x_mid,
    )
    (mid_fixed,) = call("end_fixed", end_fixed, [vec_mid], partial, other, fixing)
    other = flip(mid_fixed, 0)
    partial, turned = call(
        "start_correction", start_correction, [vec_top, ((2 * n_mid, n_top), BF16)], total, mid_fixed, transfer
    )
    (correction,) = call("end_correction", end_correction, [((rows, S, N), F32)], partial, other, turned)
    return correction, smoothed_blocks


def solution(mesh):
    n_gx, n_gy = mesh.shape["gx"], mesh.shape["gy"]
    masks = (n_gy // 2, n_gx // 2 * n_gy, n_gy // 4)
    flips = [[(source, source ^ mask) for source in range(n_gx * n_gy)] for mask in masks]
    lead = ("gx", "gy")
    in_specs = (
        P(lead, None, None),
        P(lead, None, None, None),
        P(lead, None),
        P(lead),
        P(lead, None, None),
        P(lead, None, None, None),
        P(lead, None),
        P(lead),
        P(lead, None, None),
        P(lead, None, None, None),
        P(lead, None),
    )
    out_specs = (P(lead, None, None), P(lead, None, None))
    return jax.shard_map(
        functools.partial(per_device, flips), mesh=mesh, in_specs=in_specs, out_specs=out_specs, check_vma=False
    )
```

```python
import functools

import jax
import jax.numpy as jnp
from jax import lax
from jax.experimental import pallas as pl
from jax.experimental.pallas import tpu as pltpu
from jax.sharding import PartitionSpec as P

center = 1.0
half_width = 0.6
F32 = jnp.float32
BF16 = jnp.bfloat16
N = 64
S = 8
J = 27


def chebyshev_weights():
    sigma = center / half_width
    rho = half_width / center
    weights = []
    for step in range(3):
        rho_next = 1.0 / (2.0 * sigma - rho)
        weights.append((rho_next * rho, 2.0 * rho_next / half_width))
        rho = rho_next
    return weights


W = chebyshev_weights()
COST = {"load_indices": 20000, "prepare_top": 4000, "step_first": 4000, "step_second": 100000, "step_third": 6000, "solve_mid": 20000}


def call(name, body, outs, *args, remote=(), scalars=(), scratch=(), aliases=None, limit=8):
    spaces = [
        pltpu.HBM if at in remote else pltpu.SMEM if at in scalars else pltpu.VMEM for at in range(len(args))
    ]
    args = [pltpu.with_memory_space_constraint(a, m) for a, m in zip(args, spaces)]
    places = [pltpu.SMEM if dtype == jnp.int32 else pltpu.VMEM for _, dtype in outs]
    return pl.pallas_call(
        body,
        name=name,
        out_shape=[place(shape, dtype) for place, (shape, dtype) in zip(places, outs)],
        in_specs=[pl.BlockSpec(memory_space=m) for m in spaces],
        out_specs=[pl.BlockSpec(memory_space=m) for m in places],
        scratch_shapes=scratch,
        input_output_aliases=aliases or {},
        cost_estimate=pl.CostEstimate(flops=COST.get(name, 200) * 1000000, bytes_accessed=0, transcendentals=0),
        compiler_params=pltpu.CompilerParams(vmem_limit_bytes=limit * 1024 * 1024),
    )(*args)


def copies(sources, targets, sems):
    moves = [pltpu.make_async_copy(s, t, sems.at[n]) for n, (s, t) in enumerate(zip(sources, targets))]
    for move in moves:
        move.start()

    def wait():
        for move in moves:
            move.wait()

    return wait


def split(value):
    high = value.astype(BF16)
    return high, (value - high.astype(F32)).astype(BF16)


def stack(value):
    return jnp.concatenate(split(value), axis=0)


def fold(value):
    return value[:S] + value[S:]


def apply_t(vector, matrix):
    both = stack(vector)
    both = jnp.concatenate([both, both], axis=1)
    out = lax.dot_general(both, matrix, (((1,), (1,)), ((), ())), preferred_element_type=F32)
    return fold(out)


def apply_turned(vector, matrix):
    both = stack(vector)
    both = jnp.concatenate([both, both], axis=1)
    return fold(jnp.dot(both, matrix, preferred_element_type=F32))


def apply_n(vector, matrix):
    out = fold(lax.dot_general(stack(vector), matrix, (((1,), (0,)), ((), ())), preferred_element_type=F32))
    half = out.shape[1] // 2
    return out[:, :half] + out[:, half:]


def pack(ref):
    return jnp.concatenate([ref[b] for b in range(ref.shape[0])], axis=1)


def unpack(value, ref):
    for b in range(ref.shape[0]):
        ref[b] = value[:, b * N : (b + 1) * N]


def local(index, rows, device):
    offset = index ^ (device * rows)
    return jnp.minimum(offset, rows + (offset & (rows - 1)))


def collapse_rows(cols, b, rows, device, blocks, sums):
    for part in sums:
        part[...] = jnp.zeros(part.shape, F32)
    for j in range(J):
        for n, part in enumerate(sums):
            at = local(cols[b + n, j], rows, device)
            part[at] = part[at] + blocks[b + n, j]


def pair_of(sums, at):
    return jnp.concatenate([sums[at], sums[at + 1]], axis=1)


def spread(at, rows, block):
    twice = jnp.concatenate([block, block], axis=1)
    lane = lax.broadcasted_iota(jnp.int32, (N, 2 * N), 1) // N
    return [jnp.where(lane + 2 * piece == at, twice, 0.0) for piece in range(rows)]


def put_halves(ref, rows_at, pieces):
    half = len(pieces) // 2
    width = half * 2 * N
    for p, piece in enumerate(pieces):
        high, low = split(piece)
        base = (p // half) * 2 * width + (p % half) * 2 * N
        ref[rows_at, pl.ds(base, 2 * N)] = high
        ref[rows_at, pl.ds(base + width, 2 * N)] = low


def load_indices(*refs):
    count = (len(refs) - 1) // 2
    copies(refs[:count], refs[count:-1], refs[-1])()


def prepare_top(cols, blocks, side, matrix, turned, first, product, *sums):
    rows = blocks.shape[0]
    device = cols[0, 0] // rows
    half = 2 * rows * N
    first[...] = pack(side)
    done = 0
    for b in range(0, rows, 2):
        parts = sums[b % 4 : b % 4 + 2]
        collapse_rows(cols, b, rows, device, blocks, parts)
        for n, part in enumerate(parts):
            put_halves(matrix, slice((b + n) * N, (b + n + 1) * N), [pair_of(part, 2 * c) for c in range(rows)])
        if b + 2 > rows // 2:
            product[:, done : b * N] = apply_t(first[...], matrix[done : b * N, :half])
            turned[:, done : b * N] = matrix[done : b * N, half:].T
            done = b * N
    product[:, done:] = apply_t(first[...], matrix[done:, :half])
    turned[:, done:] = matrix[done:, half:].T


def collapse_out(cols, blocks, put, sums):
    rows = blocks.shape[0]
    device = cols[0, 0] // rows
    sums = [part.at[: 2 * rows] for part in sums]
    for b in range(0, rows, 2):
        parts = sums[b % 4 : b % 4 + 2]
        collapse_rows(cols, b, rows, device, blocks, parts)
        for n, part in enumerate(parts):
            for c in range(rows):
                put(b + n, c, pair_of(part, 2 * c))


def prepare_mid(cols, agg, blocks, prolong, direction, matrix, product, send, *sums):
    product[...] = apply_t(direction[...], matrix[:, : matrix.shape[1] // 2])
    rows = blocks.shape[0]
    half = rows // 2
    n_mid = rows * N

    def put(b, c, value):
        send[c * n_mid + b * N : c * n_mid + (b + 1) * N] = value

    collapse_out(cols, blocks, put, sums)
    at = rows * n_mid
    for p in range(half):
        send[at + p * N : at + (p + 1) * N] = jnp.concatenate([prolong[2 * p], prolong[2 * p + 1]], axis=1)
    at += half * N
    device = cols[0, 0] // rows
    row = lax.broadcasted_iota(jnp.int32, (8, 2 * N), 0)
    joined = jnp.zeros((8, 2 * N), jnp.int32)
    for b in range(rows):
        joined = jnp.where(row == b, local(agg[b], half, device), joined)
    send[at : at + 8] = joined.astype(F32)


def prepare_low(
    cols, agg, blocks, prolong, direction, residual, matrix, turned, send, transfer, known, part, restrict, *sums
):
    known[...] = residual[...] - (direction[...] + apply_t(direction[...], matrix[:, : matrix.shape[1] // 2]))
    n_low = blocks.shape[0] * N

    def put(b, c, value):
        send[c * n_low + b * N : c * n_low + (b + 1) * N] = value

    collapse_out(cols, blocks, put, sums)
    rows = prolong.shape[0]
    device = cols[0, 0] // blocks.shape[0]
    for b in range(rows):
        at = local(agg[b], rows // 2, device)
        put_halves(transfer, slice(b * N, (b + 1) * N), spread(at, rows // 2, prolong[b]))
    half = transfer.shape[1] // 2
    part[...] = apply_n(known[...], transfer[:, half:])
    depth = turned.shape[0] // 2
    high, low = split(
        multiply(
            (turned[:depth], turned[depth:]), (transfer[:, half : half + half // 2], transfer[:, half + half // 2 :])
        )
    )
    restrict[:depth] = high
    restrict[depth:] = low


def step_first(first, product, other, turned, direction, residual):
    d = first[...]
    r = d - (d + product[...] + apply_turned(pack(other), turned[...]))
    residual[...] = r
    direction[...] = W[0][0] * d + W[0][1] * r


def step_second(first, old, residual, product, other, turned, direction, new_residual, total):
    d = old[...]
    r = residual[...] - (d + product[...] + apply_turned(other[...], turned[...]))
    new_residual[...] = r
    new = W[1][0] * d + W[1][1] * r
    direction[...] = new
    total[...] = first[...] + d + new


def step_third(part, other, restrict, other_part):
    other_part[...] = part[...] - apply_turned(other[...], restrict[...])


def restrict_own(known, other, turned, transfer_top, source, own_part, out, matrix, transfer):
    r = known[...] - apply_turned(other[...], turned[...])
    own_part[...] = apply_n(r, transfer_top[:, : transfer_top.shape[1] // 2])
    unpack(r, out)
    join_mid(source, matrix, transfer, False)


def add_mid(a, b, after, out):
    out[...] = a[...] + b[...]


def own_mid(side, matrix, low, product, low_out):
    product[...] = apply_turned(side[...], matrix[: matrix.shape[0] // 2])


def join_mid(source, matrix, transfer, turn):
    n_mid = matrix.shape[1]
    rows = n_mid // N
    half = rows // 2
    for c in range(rows):
        to = (c + half) % rows if turn else c
        high, low = split(source[c * n_mid : (c + 1) * n_mid].T)
        base = (to // half) * 2 * n_mid + (to % half) * 2 * N
        matrix[base : base + 2 * N] = high
        matrix[base + n_mid : base + n_mid + 2 * N] = low
    at = rows * n_mid
    joined = at + half * N
    for b in range(rows):
        both = source[at + (b // 2) * N : at + (b // 2 + 1) * N]
        block = both[:, (b % 2) * N : (b % 2 + 1) * N]
        to = source[joined + b : joined + b + 1].astype(jnp.int32)
        pieces = spread(to, half, block)
        for p, piece in enumerate(pieces):
            put = (p + half // 2) % half if turn else p
            high, low = split(piece)
            matrix_rows = slice(b * N, (b + 1) * N)
            transfer[matrix_rows, put * 2 * N : (put + 1) * 2 * N] = high
            transfer[matrix_rows, n_mid + put * 2 * N : n_mid + (put + 1) * 2 * N] = low


def join_other(source, side, own, matrix, transfer, product):
    join_mid(source, matrix, transfer, True)
    other = apply_turned(side[...], matrix[: matrix.shape[0] // 2])
    product[...] = jnp.concatenate([own[...], other], axis=1)


def multiply(a, b):
    (a_high, a_low), (b_high, b_low) = a, b
    out = jnp.dot(a_high, b_high, preferred_element_type=F32)
    out += jnp.dot(a_high, b_low, preferred_element_type=F32)
    return out + jnp.dot(a_low, b_high, preferred_element_type=F32)


def compose_low(own, other, out):
    half = own.shape[0] // 2
    top = jnp.concatenate([own[:half], own[half:]], axis=1)
    low = jnp.concatenate([other[half:], other[:half]], axis=1)
    pair = jnp.concatenate([top, low], axis=0)
    (a0, b0), (a1, b1) = W[0], W[1]
    square = multiply(split(top), split(pair))
    row = lax.broadcasted_iota(jnp.int32, top.shape, 0)
    column = lax.broadcasted_iota(jnp.int32, top.shape, 1)
    value = jnp.where(row == column, 1.0 + (1.0 + a1 - b1) * a0, 0.0)
    value += (b1 * (b0 - 1.0 - a0) - (1.0 + a1) * b0) * top + (b1 * b0) * square
    out[:half] = value[:, :half]
    out[half:] = value[:, half:]


def compose_fixed(own, other, transfer, pair, fine, partial, matrix):
    half = own.shape[0] // 2
    width = 2 * half
    near, far = [], []
    for at, source in ((0, own), (1, other)):
        solve = jnp.concatenate([source[:half], source[half:]], axis=1)
        here = transfer[:, at * half : (at + 1) * half], transfer[:, width + at * half : width + (at + 1) * half]
        product = multiply(here, split(solve))
        near.append(product[:, :half])
        far.append(product[:, half:])
    partial[...] = fine[...] + apply_t(pair[...], jnp.concatenate(split(jnp.concatenate(near, axis=1)), axis=1))
    high, low = split(jnp.concatenate(far, axis=1).T)
    matrix[:width] = high
    matrix[width:] = low


def solve_mid(product, own, other, matrix_own, matrix_other, transfer_own, transfer_other, low_pair, solution):
    half = own.shape[1]
    mid = matrix_own.shape[0] // 2

    def pair_product(value, columns):
        return jnp.concatenate(
            [apply_turned(value, matrix_own[columns]), apply_turned(value, matrix_other[columns])], axis=1
        )

    d = jnp.concatenate([own[...], other[...]], axis=1)
    r = d - (d + product[...] + pair_product(other[...], slice(mid, 2 * mid)))
    x = d[:, :half]
    for step in range(2):
        d = W[step][0] * d + W[step][1] * r
        x = x + d[:, :half]
        r = r - (d + pair_product(d[:, :half], slice(0, mid)) + pair_product(d[:, half:], slice(mid, 2 * mid)))
    solution[...] = x
    low_pair[...] = apply_n(r[:, :half], transfer_own[...]) + apply_n(r[:, half:], transfer_other[...])


def end_fixed(partial, other, matrix, fixed):
    fixed[...] = partial[...] + apply_turned(other[...], matrix[...])


def start_correction(total, fixed, transfer, out, turned):
    half = transfer.shape[1] // 2
    turned[...] = transfer[:, half:].T
    out[...] = total[...] + apply_t(fixed[...], transfer[:, :half])


def end_correction(partial, other, turned, out):
    unpack(partial[...] + apply_turned(other[...], turned[...]), out)


def per_device(
    flips,
    right_side,
    operator_top,
    columns_top,
    aggregate_top,
    prolong_top,
    operator_mid,
    columns_mid,
    aggregate_mid,
    prolong_mid,
    operator_low,
    columns_low,
):
    def flip(value, level):
        return lax.ppermute(value, ("gx", "gy"), flips[level])

    rows = operator_top.shape[0]
    n_top = rows * N
    n_mid = n_top // 2
    n_low = n_mid // 2
    vec_top = ((S, n_top), F32)
    vec_mid = ((S, n_mid), F32)
    sums = [pltpu.VMEM((2 * rows, N, N), F32)] * 4
    mid_pieces = ((rows // 2 * n_mid + rows // 4 * N + 8, 2 * N), F32)
    low_pieces = ((rows // 4 * n_low, 2 * N), F32)

    other = flip(right_side, 0)
    indices = (columns_top, aggregate_top, columns_mid, aggregate_mid, columns_low)
    cols_top, agg_top, cols_mid, agg_mid, cols_low = call(
        "load_indices",
        load_indices,
        [(a.shape, jnp.int32) for a in indices],
        *indices,
        remote=range(5),
        scratch=[pltpu.SemaphoreType.DMA((5,))],
    )
    matrix, turned, first, product = call(
        "prepare_top",
        prepare_top,
        [((n_top, 4 * n_top), BF16), ((2 * n_top, n_top), BF16), vec_top, vec_top],
        cols_top,
        operator_top,
        right_side,
        scalars=(0,),
        scratch=sums,
    )
    d1, r1 = call("step_first", step_first, [vec_top, vec_top], first, product, other, turned)
    other = flip(d1, 0)
    product, send_mid = call(
        "prepare_mid",
        prepare_mid,
        [vec_top, mid_pieces],
        cols_mid,
        agg_mid,
        operator_mid,
        prolong_mid,
        d1,
        matrix,
        scalars=(0, 1),
        scratch=sums,
    )
    mid_arrived = flip(send_mid, 1)
    d2, r2, total = call("step_second", step_second, [vec_top] * 3, first, d1, r1, product, other, turned)
    other = flip(d2, 0)
    send_low, transfer, known, part, restrict = call(
        "prepare_low",
        prepare_low,
        [low_pieces, ((n_top, 4 * n_mid), BF16), vec_top, vec_mid, ((2 * n_top, n_mid), BF16)],
        cols_low,
        agg_top,
        operator_low,
        prolong_top,
        d2,
        r2,
        matrix,
        turned,
        scalars=(0, 1),
        scratch=sums,
    )
    low_arrived = flip(send_low, 2)
    (other_part,) = call("step_third", step_third, [vec_mid], part, other, restrict)
    arrived = flip(other_part, 0)
    own_part, smoothed_blocks, mid_own, transfer_own = call(
        "restrict_own",
        restrict_own,
        [vec_mid, ((rows, S, N), F32), ((4 * n_mid, n_mid), BF16), ((n_mid, 4 * n_low), BF16)],
        known,
        other,
        turned,
        transfer,
        send_mid,
    )
    (solve_own,) = call("compose_low", compose_low, [low_pieces], send_low, low_arrived)
    (mid_side,) = call("add_mid", add_mid, [vec_mid], own_part, arrived, solve_own)
    other = flip(mid_side, 1)
    product, solve_own = call("own_mid", own_mid, [vec_mid, low_pieces], mid_side, mid_own, solve_own, aliases={2: 1})
    solve_other = flip(solve_own, 1)
    mid_other, transfer_other, product = call(
        "join_other",
        join_other,
        [((4 * n_mid, n_mid), BF16), ((n_mid, 4 * n_low), BF16), vec_top],
        mid_arrived,
        mid_side,
        product,
    )
    low_pair, x_mid = call(
        "solve_mid",
        solve_mid,
        [((S, 2 * n_low), F32), vec_mid],
        product,
        mid_side,
        other,
        mid_own,
        mid_other,
        transfer_own,
        transfer_other,
    )
    other = flip(low_pair, 2)
    partial, fixing = call(
        "compose_fixed",
        compose_fixed,
        [vec_mid, ((4 * n_low, n_mid), BF16)],
        solve_own,
        solve_other,
        transfer_own,
        low_pair,
        x_mid,
    )
    (mid_fixed,) = call("end_fixed", end_fixed, [vec_mid], partial, other, fixing)
    other = flip(mid_fixed, 0)
    partial, turned = call(
        "start_correction", start_correction, [vec_top, ((2 * n_mid, n_top), BF16)], total, mid_fixed, transfer
    )
    (correction,) = call("end_correction", end_correction, [((rows, S, N), F32)], partial, other, turned)
    return correction, smoothed_blocks


def solution(mesh):
    n_gx, n_gy = mesh.shape["gx"], mesh.shape["gy"]
    masks = (n_gy // 2, n_gx // 2 * n_gy, n_gy // 4)
    flips = [[(source, source ^ mask) for source in range(n_gx * n_gy)] for mask in masks]
    lead = ("gx", "gy")
    in_specs = (
        P(lead, None, None),
        P(lead, None, None, None),
        P(lead, None),
        P(lead),
        P(lead, None, None),
        P(lead, None, None, None),
        P(lead, None),
        P(lead),
        P(lead, None, None),
        P(lead, None, None, None),
        P(lead, None),
    )
    out_specs = (P(lead, None, None), P(lead, None, None))
    return jax.shard_map(
        functools.partial(per_device, flips), mesh=mesh, in_specs=in_specs, out_specs=out_specs, check_vma=False
    )
```

```python
import functools

import jax
import jax.numpy as jnp
from jax import lax
from jax.experimental import pallas as pl
from jax.experimental.pallas import tpu as pltpu
from jax.sharding import PartitionSpec as P

center = 1.0
half_width = 0.6
F32 = jnp.float32
BF16 = jnp.bfloat16
N = 64
S = 8
J = 27


def chebyshev_weights():
    sigma = center / half_width
    rho = half_width / center
    weights = []
    for step in range(3):
        rho_next = 1.0 / (2.0 * sigma - rho)
        weights.append((rho_next * rho, 2.0 * rho_next / half_width))
        rho = rho_next
    return weights


W = chebyshev_weights()
COST = {"load_indices": 20000, "prepare_top": 4000, "step_first": 4000, "step_second": 100000, "step_third": 6000, "solve_mid": 20000}


def call(name, body, outs, *args, remote=(), scalars=(), scratch=(), aliases=None, limit=8):
    spaces = [
        pltpu.HBM if at in remote else pltpu.SMEM if at in scalars else pltpu.VMEM for at in range(len(args))
    ]
    args = [pltpu.with_memory_space_constraint(a, m) for a, m in zip(args, spaces)]
    places = [pltpu.SMEM if dtype == jnp.int32 else pltpu.VMEM for _, dtype in outs]
    return pl.pallas_call(
        body,
        name=name,
        out_shape=[place(shape, dtype) for place, (shape, dtype) in zip(places, outs)],
        in_specs=[pl.BlockSpec(memory_space=m) for m in spaces],
        out_specs=[pl.BlockSpec(memory_space=m) for m in places],
        scratch_shapes=scratch,
        input_output_aliases=aliases or {},
        cost_estimate=pl.CostEstimate(flops=COST.get(name, 200) * 1000000, bytes_accessed=0, transcendentals=0),
        compiler_params=pltpu.CompilerParams(vmem_limit_bytes=limit * 1024 * 1024),
    )(*args)


def copies(sources, targets, sems):
    moves = [pltpu.make_async_copy(s, t, sems.at[n]) for n, (s, t) in enumerate(zip(sources, targets))]
    for move in moves:
        move.start()

    def wait():
        for move in moves:
            move.wait()

    return wait


def split(value):
    high = value.astype(BF16)
    return high, (value - high.astype(F32)).astype(BF16)


def stack(value):
    return jnp.concatenate(split(value), axis=0)


def fold(value):
    return value[:S] + value[S:]


def apply_t(vector, matrix):
    both = stack(vector)
    both = jnp.concatenate([both, both], axis=1)
    out = lax.dot_general(both, matrix, (((1,), (1,)), ((), ())), preferred_element_type=F32)
    return fold(out)


def apply_turned(vector, matrix):
    both = stack(vector)
    both = jnp.concatenate([both, both], axis=1)
    return fold(jnp.dot(both, matrix, preferred_element_type=F32))


def apply_n(vector, matrix):
    out = fold(lax.dot_general(stack(vector), matrix, (((1,), (0,)), ((), ())), preferred_element_type=F32))
    half = out.shape[1] // 2
    return out[:, :half] + out[:, half:]


def pack(ref):
    return jnp.concatenate([ref[b] for b in range(ref.shape[0])], axis=1)


def unpack(value, ref):
    for b in range(ref.shape[0]):
        ref[b] = value[:, b * N : (b + 1) * N]


def local(index, rows, device):
    offset = index ^ (device * rows)
    return jnp.minimum(offset, rows + (offset & (rows - 1)))


def collapse_rows(cols, b, rows, device, blocks, sums):
    for part in sums:
        part[...] = jnp.zeros(part.shape, F32)
    for j in range(J):
        for n, part in enumerate(sums):
            at = local(cols[b + n, j], rows, device)
            part[at] = part[at] + blocks[b + n, j]


def pair_of(sums, at):
    return jnp.concatenate([sums[at], sums[at + 1]], axis=1)


def spread(at, rows, block):
    twice = jnp.concatenate([block, block], axis=1)
    lane = lax.broadcasted_iota(jnp.int32, (N, 2 * N), 1) // N
    return [jnp.where(lane + 2 * piece == at, twice, 0.0) for piece in range(rows)]


def put_halves(ref, rows_at, pieces):
    half = len(pieces) // 2
    width = half * 2 * N
    for p, piece in enumerate(pieces):
        high, low = split(piece)
        base = (p // half) * 2 * width + (p % half) * 2 * N
        ref[rows_at, pl.ds(base, 2 * N)] = high
        ref[rows_at, pl.ds(base + width, 2 * N)] = low


def load_indices(*refs):
    count = (len(refs) - 1) // 2
    copies(refs[:count], refs[count:-1], refs[-1])()


def prepare_top(cols, blocks, side, matrix, turned, first, product, *sums):
    rows = blocks.shape[0]
    device = cols[0, 0] // rows
    half = 2 * rows * N
    first[...] = pack(side)
    done = 0
    for b in range(0, rows, 2):
        parts = sums[b % 4 : b % 4 + 2]
        collapse_rows(cols, b, rows, device, blocks, parts)
        for n, part in enumerate(parts):
            put_halves(matrix, slice((b + n) * N, (b + n + 1) * N), [pair_of(part, 2 * c) for c in range(rows)])
        if b + 2 > rows // 2:
            product[:, done : b * N] = apply_t(first[...], matrix[done : b * N, :half])
            turned[:, done : b * N] = matrix[done : b * N, half:].T
            done = b * N
    product[:, done:] = apply_t(first[...], matrix[done:, :half])
    turned[:, done:] = matrix[done:, half:].T


def collapse_out(cols, blocks, put, sums):
    rows = blocks.shape[0]
    device = cols[0, 0] // rows
    sums = [part.at[: 2 * rows] for part in sums]
    for b in range(0, rows, 2):
        parts = sums[b % 4 : b % 4 + 2]
        collapse_rows(cols, b, rows, device, blocks, parts)
        for n, part in enumerate(parts):
            for c in range(rows):
                put(b + n, c, pair_of(part, 2 * c))


def prepare_mid(cols, agg, blocks, prolong, direction, matrix, product, send, *sums):
    product[...] = apply_t(direction[...], matrix[:, : matrix.shape[1] // 2])
    rows = blocks.shape[0]
    half = rows // 2
    n_mid = rows * N

    def put(b, c, value):
        send[c * n_mid + b * N : c * n_mid + (b + 1) * N] = value

    collapse_out(cols, blocks, put, sums)
    at = rows * n_mid
    for p in range(half):
        send[at + p * N : at + (p + 1) * N] = jnp.concatenate([prolong[2 * p], prolong[2 * p + 1]], axis=1)
    at += half * N
    device = cols[0, 0] // rows
    row = lax.broadcasted_iota(jnp.int32, (8, 2 * N), 0)
    joined = jnp.zeros((8, 2 * N), jnp.int32)
    for b in range(rows):
        joined = jnp.where(row == b, local(agg[b], half, device), joined)
    send[at : at + 8] = joined.astype(F32)


def prepare_low(
    cols, agg, blocks, prolong, direction, residual, matrix, turned, send, transfer, known, part, restrict, *sums
):
    known[...] = residual[...] - (direction[...] + apply_t(direction[...], matrix[:, : matrix.shape[1] // 2]))
    n_low = blocks.shape[0] * N

    def put(b, c, value):
        send[c * n_low + b * N : c * n_low + (b + 1) * N] = value

    collapse_out(cols, blocks, put, sums)
    rows = prolong.shape[0]
    device = cols[0, 0] // blocks.shape[0]
    for b in range(rows):
        at = local(agg[b], rows // 2, device)
        put_halves(transfer, slice(b * N, (b + 1) * N), spread(at, rows // 2, prolong[b]))
    half = transfer.shape[1] // 2
    part[...] = apply_n(known[...], transfer[:, half:])
    depth = turned.shape[0] // 2
    high, low = split(
        multiply(
            (turned[:depth], turned[depth:]), (transfer[:, half : half + half // 2], transfer[:, half + half // 2 :])
        )
    )
    restrict[:depth] = high
    restrict[depth:] = low


def step_first(first, product, other, turned, direction, residual):
    d = first[...]
    r = d - (d + product[...] + apply_turned(pack(other), turned[...]))
    residual[...] = r
    direction[...] = W[0][0] * d + W[0][1] * r


def step_second(first, old, residual, product, other, turned, direction, new_residual, total):
    d = old[...]
    r = residual[...] - (d + product[...] + apply_turned(other[...], turned[...]))
    new_residual[...] = r
    new = W[1][0] * d + W[1][1] * r
    direction[...] = new
    total[...] = first[...] + d + new


def step_third(part, other, restrict, other_part):
    other_part[...] = part[...] - apply_turned(other[...], restrict[...])


def restrict_own(known, other, turned, transfer_top, source, own_part, out, matrix, transfer):
    r = known[...] - apply_turned(other[...], turned[...])
    own_part[...] = apply_n(r, transfer_top[:, : transfer_top.shape[1] // 2])
    unpack(r, out)
    join_mid(source, matrix, transfer, 0)


def add_mid(a, b, after, out):
    out[...] = a[...] + b[...]


def own_mid(side, matrix, low, product, low_out):
    product[...] = apply_turned(side[...], matrix[: matrix.shape[0] // 2, : matrix.shape[1] // 2])


def join_mid(source, matrix, transfer, turn):
    n_mid = matrix.shape[1] // 2
    rows = n_mid // N
    half = rows // 2
    here = slice(turn * n_mid, (turn + 1) * n_mid)
    for c in range(rows):
        to = (c + half) % rows if turn else c
        high, low = split(source[c * n_mid : (c + 1) * n_mid].T)
        base = (to // half) * 2 * n_mid + (to % half) * 2 * N
        matrix[base : base + 2 * N, here] = high
        matrix[base + n_mid : base + n_mid + 2 * N, here] = low
    at = rows * n_mid
    joined = at + half * N
    for b in range(rows):
        both = source[at + (b // 2) * N : at + (b // 2 + 1) * N]
        block = both[:, (b % 2) * N : (b % 2 + 1) * N]
        to = source[joined + b : joined + b + 1].astype(jnp.int32)
        pieces = spread(to, half, block)
        for p, piece in enumerate(pieces):
            put = (p + half // 2) % half if turn else p
            high, low = split(piece)
            matrix_rows = slice(turn * n_mid + b * N, turn * n_mid + (b + 1) * N)
            transfer[matrix_rows, put * 2 * N : (put + 1) * 2 * N] = high
            transfer[matrix_rows, n_mid + put * 2 * N : n_mid + (put + 1) * 2 * N] = low


def join_other(source, side, own, matrix_in, transfer_in, matrix, transfer, product, last):
    join_mid(source, matrix, transfer, 1)
    other = apply_turned(side[...], matrix[: matrix.shape[0] // 2, matrix.shape[1] // 2 :])
    product[...] = jnp.concatenate([own[...], other], axis=1)
    n_mid = matrix.shape[1] // 2
    for at in (0, 2 * n_mid):
        here = matrix[at : at + n_mid], matrix[at + n_mid : at + 2 * n_mid]
        high, low = split(multiply(here, (transfer[:, :n_mid], transfer[:, n_mid:])))
        last[at : at + n_mid] = high
        last[at + n_mid : at + 2 * n_mid] = low


def multiply(a, b):
    (a_high, a_low), (b_high, b_low) = a, b
    out = jnp.dot(a_high, b_high, preferred_element_type=F32)
    out += jnp.dot(a_high, b_low, preferred_element_type=F32)
    return out + jnp.dot(a_low, b_high, preferred_element_type=F32)


def compose_low(own, other, out):
    half = own.shape[0] // 2
    top = jnp.concatenate([own[:half], own[half:]], axis=1)
    low = jnp.concatenate([other[half:], other[:half]], axis=1)
    pair = jnp.concatenate([top, low], axis=0)
    (a0, b0), (a1, b1) = W[0], W[1]
    square = multiply(split(top), split(pair))
    row = lax.broadcasted_iota(jnp.int32, top.shape, 0)
    column = lax.broadcasted_iota(jnp.int32, top.shape, 1)
    value = jnp.where(row == column, 1.0 + (1.0 + a1 - b1) * a0, 0.0)
    value += (b1 * (b0 - 1.0 - a0) - (1.0 + a1) * b0) * top + (b1 * b0) * square
    out[:half] = value[:, :half]
    out[half:] = value[:, half:]


def compose_fixed(own, other, transfer, pair, fine, partial, matrix):
    half = own.shape[0] // 2
    width = 2 * half
    near, far = [], []
    for at, source in ((0, own), (1, other)):
        solve = jnp.concatenate([source[:half], source[half:]], axis=1)
        rows = slice(0, fine.shape[1])
        here = tuple(transfer[rows, low + at * half : low + (at + 1) * half] for low in (0, width))
        product = multiply(here, split(solve))
        near.append(product[:, :half])
        far.append(product[:, half:])
    partial[...] = fine[...] + apply_t(pair[...], jnp.concatenate(split(jnp.concatenate(near, axis=1)), axis=1))
    high, low = split(jnp.concatenate(far, axis=1).T)
    matrix[:width] = high
    matrix[width:] = low


def solve_mid(product, own, other, matrix, transfer, last, low_pair, solution):
    half = own.shape[1]

    def pair_product(value, by):
        near, far = stack(value[:, :half]), stack(value[:, half:])
        both = jnp.concatenate([near, near, far, far], axis=1)
        return fold(jnp.dot(both, by[...], preferred_element_type=F32))

    d = jnp.concatenate([own[...], other[...]], axis=1)
    r = d - (d + product[...] + apply_turned(other[...], matrix[matrix.shape[0] // 2 :]))
    x = d[:, :half]
    d = W[0][0] * d + W[0][1] * r
    x = x + d[:, :half]
    r = r - (d + pair_product(d, matrix))
    d = W[1][0] * d + W[1][1] * r
    solution[...] = x + d[:, :half]
    low_pair[...] = apply_n(r - d, transfer[...]) - pair_product(d, last)


def end_fixed(partial, other, matrix, fixed):
    fixed[...] = partial[...] + apply_turned(other[...], matrix[...])


def start_correction(total, fixed, transfer, out, turned):
    half = transfer.shape[1] // 2
    turned[...] = transfer[:, half:].T
    out[...] = total[...] + apply_t(fixed[...], transfer[:, :half])


def end_correction(partial, other, turned, out):
    unpack(partial[...] + apply_turned(other[...], turned[...]), out)


def per_device(
    flips,
    right_side,
    operator_top,
    columns_top,
    aggregate_top,
    prolong_top,
    operator_mid,
    columns_mid,
    aggregate_mid,
    prolong_mid,
    operator_low,
    columns_low,
):
    def flip(value, level):
        return lax.ppermute(value, ("gx", "gy"), flips[level])

    rows = operator_top.shape[0]
    n_top = rows * N
    n_mid = n_top // 2
    n_low = n_mid // 2
    vec_top = ((S, n_top), F32)
    vec_mid = ((S, n_mid), F32)
    sums = [pltpu.VMEM((2 * rows, N, N), F32)] * 4
    mid_pieces = ((rows // 2 * n_mid + rows // 4 * N + 8, 2 * N), F32)
    low_pieces = ((rows // 4 * n_low, 2 * N), F32)

    other = flip(right_side, 0)
    indices = (columns_top, aggregate_top, columns_mid, aggregate_mid, columns_low)
    cols_top, agg_top, cols_mid, agg_mid, cols_low = call(
        "load_indices",
        load_indices,
        [(a.shape, jnp.int32) for a in indices],
        *indices,
        remote=range(5),
        scratch=[pltpu.SemaphoreType.DMA((5,))],
    )
    matrix, turned, first, product = call(
        "prepare_top",
        prepare_top,
        [((n_top, 4 * n_top), BF16), ((2 * n_top, n_top), BF16), vec_top, vec_top],
        cols_top,
        operator_top,
        right_side,
        scalars=(0,),
        scratch=sums,
    )
    d1, r1 = call("step_first", step_first, [vec_top, vec_top], first, product, other, turned)
    other = flip(d1, 0)
    product, send_mid = call(
        "prepare_mid",
        prepare_mid,
        [vec_top, mid_pieces],
        cols_mid,
        agg_mid,
        operator_mid,
        prolong_mid,
        d1,
        matrix,
        scalars=(0, 1),
        scratch=sums,
    )
    mid_arrived = flip(send_mid, 1)
    d2, r2, total = call("step_second", step_second, [vec_top] * 3, first, d1, r1, product, other, turned)
    other = flip(d2, 0)
    send_low, transfer, known, part, restrict = call(
        "prepare_low",
        prepare_low,
        [low_pieces, ((n_top, 4 * n_mid), BF16), vec_top, vec_mid, ((2 * n_top, n_mid), BF16)],
        cols_low,
        agg_top,
        operator_low,
        prolong_top,
        d2,
        r2,
        matrix,
        turned,
        scalars=(0, 1),
        scratch=sums,
    )
    low_arrived = flip(send_low, 2)
    (other_part,) = call("step_third", step_third, [vec_mid], part, other, restrict)
    arrived = flip(other_part, 0)
    own_part, smoothed_blocks, mid_matrix, mid_transfer = call(
        "restrict_own",
        restrict_own,
        [vec_mid, ((rows, S, N), F32), ((4 * n_mid, 2 * n_mid), BF16), ((2 * n_mid, 4 * n_low), BF16)],
        known,
        other,
        turned,
        transfer,
        send_mid,
    )
    (solve_own,) = call("compose_low", compose_low, [low_pieces], send_low, low_arrived)
    (mid_side,) = call("add_mid", add_mid, [vec_mid], own_part, arrived, solve_own)
    other = flip(mid_side, 1)
    product, solve_own = call("own_mid", own_mid, [vec_mid, low_pieces], mid_side, mid_matrix, solve_own, aliases={2: 1})
    solve_other = flip(solve_own, 1)
    mid_matrix, mid_transfer, product, last = call(
        "join_other",
        join_other,
        [((4 * n_mid, 2 * n_mid), BF16), ((2 * n_mid, 4 * n_low), BF16), vec_top, ((4 * n_mid, n_mid), BF16)],
        mid_arrived,
        mid_side,
        product,
        mid_matrix,
        mid_transfer,
        aliases={3: 0, 4: 1},
    )
    low_pair, x_mid = call(
        "solve_mid",
        solve_mid,
        [((S, 2 * n_low), F32), vec_mid],
        product,
        mid_side,
        other,
        mid_matrix,
        mid_transfer,
        last,
    )
    other = flip(low_pair, 2)
    partial, fixing = call(
        "compose_fixed",
        compose_fixed,
        [vec_mid, ((4 * n_low, n_mid), BF16)],
        solve_own,
        solve_other,
        mid_transfer,
        low_pair,
        x_mid,
    )
    (mid_fixed,) = call("end_fixed", end_fixed, [vec_mid], partial, other, fixing)
    other = flip(mid_fixed, 0)
    partial, turned = call(
        "start_correction", start_correction, [vec_top, ((2 * n_mid, n_top), BF16)], total, mid_fixed, transfer
    )
    (correction,) = call("end_correction", end_correction, [((rows, S, N), F32)], partial, other, turned)
    return correction, smoothed_blocks


def solution(mesh):
    n_gx, n_gy = mesh.shape["gx"], mesh.shape["gy"]
    masks = (n_gy // 2, n_gx // 2 * n_gy, n_gy // 4)
    flips = [[(source, source ^ mask) for source in range(n_gx * n_gy)] for mask in masks]
    lead = ("gx", "gy")
    in_specs = (
        P(lead, None, None),
        P(lead, None, None, None),
        P(lead, None),
        P(lead),
        P(lead, None, None),
        P(lead, None, None, None),
        P(lead, None),
        P(lead),
        P(lead, None, None),
        P(lead, None, None, None),
        P(lead, None),
    )
    out_specs = (P(lead, None, None), P(lead, None, None))
    return jax.shard_map(
        functools.partial(per_device, flips), mesh=mesh, in_specs=in_specs, out_specs=out_specs, check_vma=False
    )
```
